512 devices in a mesh: rep: 16 (over y, x), fsdp: 32 (over z, core).
Axes of the slice: x: 4, y: 4, z: 16, core: 2. Of those that a mesh axis runs over, the one named last changes fastest.
Arguments:
- partials: float32 [16, 32, 64, 4096], P('rep', 'fsdp'), may hold values from -6 to 6
- owner_blocks: int32 [32], replicated, may hold values from 1 to 512, 4096 in all
- momentum: float32 [16, 64, 16384], P('rep', None, 'fsdp'), may hold values from -6 to 6
- weights: float32 [64, 16384], P(None, 'fsdp'), may hold values from -6 to 6
- selected: int32 [16, 32, 16384], P(None, None, 'fsdp'), may hold values from 0 to 63, as said below
Outputs:
- new_momentum: float32 [16, 64, 16384], P('rep', None, 'fsdp')
- new_weights: float32 [64, 16384], P(None, 'fsdp')
The draws below stay inside these ranges and needn't reach their ends.
Inputs may be any that keep to these rules, and one draw needn't show every extreme that they name: `owner_blocks`: counts of the 32 owners sum to 4096; the largest is exactly 512. `selected`: for each group and slot the 32 listed numbers are distinct; lists of slots that are not live are ignored.
All inputs are finite; a program needn't handle non-finite values.
Results may differ from the reference program's by a relative error of at most 0.00005.
Values sent between devices are 32-bit elements; how exact they have to be, the bound alone decides.
No kernel may reach another device: no remote copies, remote signals or barrier semaphores. Data moves between devices by JAX's collectives and lax.ppermute only.
A program may use at most 64 MiB of HBM per device.

```python
import math
import jax
import jax.numpy as jnp
import numpy as np
from jax import lax

BLOCK = 64
K = 32
BLOCKS = 4096
MOST = 512
SLOTS = 16384
N_REP = 16
N_FSDP = 32


def draw_selected(key, part):
    key = jax.random.fold_in(key, 7)
    scores = jax.random.randint(key, (N_REP, BLOCK, SLOTS), 0, 1 << 20, dtype=jnp.int32)
    scores = scores * BLOCK + jnp.arange(BLOCK, dtype=jnp.int32)[None, :, None]
    order = jnp.argsort(scores, axis=1, stable=True)
    return order[:, :K, :].astype(jnp.int32)


def with_spikes(entries, key, source, target, shards_of, factor):
    owner, partner = [(jnp.arange(entries.shape[axis_at]) // (entries.shape[axis_at] // shards_of)).reshape([-1 if axis == axis_at else 1 for axis in range(entries.ndim)]) for axis_at in (source, target)]
    chosen = jax.random.permutation(key, shards_of)[partner]
    strong = (owner == chosen) | (owner == (partner + shards_of // 2) % shards_of)
    return jnp.where(strong, factor * entries, entries)


def shard_levels(own_key, shape, pieces, smallest, largest):
    def one(dim, shards_of):
        draws = jax.random.uniform(jax.random.fold_in(jax.random.fold_in(own_key, 6), dim), (shards_of,), jnp.float32, smallest / len(pieces), largest / len(pieces))
        return jnp.repeat(jnp.exp(draws), shape[dim] // shards_of).reshape((-1,) + (1,) * (len(shape) - dim - 1))

    loudness = one(*pieces[0])
    for cut in pieces[1:]:
        loudness = loudness * one(*cut)
    return loudness


def length_profile(count, total, reach, skew):
    loads = [(1 << 20) // math.isqrt(grade ** skew) + 1 for grade in range(2, count + 1)]
    rest, holding = total - reach - (count - 1), [1] * (count - 1)
    while rest > 0:
        free = [i for i in range(count - 1) if holding[i] < reach]
        mass, remaining = sum([loads[i] for i in free]), rest
        for i in free:
            extra = min(reach - holding[i], max(1, remaining * loads[i] // mass), rest)
            holding[i] = holding[i] + extra
            rest = rest - extra
    return np.array([reach] + holding)


def uneven_parts(stream_key, amount, total, bound, lean):
    if amount == 2:
        one = jax.random.randint(stream_key, (), max(1, total - bound), min(bound, total - 1) + 1)
        return jnp.stack([one, total - one])
    sizes = jnp.asarray(length_profile(amount, total, bound, lean), jnp.int32)
    twos = (amount - 1) // 2
    donor, receiver = sizes[1:1 + 2 * twos:2], sizes[2:2 + 2 * twos:2]
    room = jnp.minimum(donor - 1, bound - receiver)
    passed = jax.random.randint(jax.random.fold_in(stream_key, 1), (twos,), 0, 1 << 20) % (room + 1)
    sizes = sizes.at[1:1 + 2 * twos:2].set(donor - passed).at[2:2 + 2 * twos:2].set(receiver + passed)
    return sizes[jax.random.permutation(jax.random.fold_in(stream_key, 2), amount)]


def centred(stream_key, shape, scale, reach, pieces=(), held_as=jnp.bfloat16):
    drawn = scale * jax.random.normal(stream_key, shape, jnp.float32)
    if pieces:
        drawn = drawn * shard_levels(stream_key, shape, pieces, -0.22, 0.18)
    return jnp.clip(drawn, -reach, reach).astype(held_as)


def bell_draw_with(rng, dims, width, bound, pieces, heavy, held_as=jnp.bfloat16):
    drawn = width * jax.random.normal(rng, dims, jnp.float32)
    if pieces:
        drawn = drawn * shard_levels(rng, dims, pieces, -0.22, 0.18)
    return jnp.clip(with_spikes(drawn, jax.random.fold_in(rng, 3), *heavy), -bound, bound).astype(held_as)


def setup_inputs(seed: int = 0) -> dict:
    arg_keys = jax.random.split(jax.random.key(seed), 6)
    partials = bell_draw_with(arg_keys[0], (N_REP, N_FSDP, BLOCK, BLOCKS), 1.0, 6.0, ((0, 16), (1, 32)), (1, 3, 32, 2.75), jnp.float32)
    owner_blocks = uneven_parts(arg_keys[1], N_FSDP, BLOCKS, MOST, 2).astype(jnp.int32)
    momentum = centred(arg_keys[2], (N_REP, BLOCK, SLOTS), 1.0, 6.0, ((0, 16), (2, 32)), jnp.float32)
    weights = centred(arg_keys[3], (BLOCK, SLOTS), 1.0, 6.0, ((1, 32),), jnp.float32)
    selected = draw_selected(jax.random.fold_in(arg_keys[5], 71), 0)
    return dict(partials=partials, owner_blocks=owner_blocks, momentum=momentum, weights=weights, selected=selected)


momentum_decay = 0.9
step_rate = 0.5

def dct_matrix():
    row_index = jnp.arange(BLOCK, dtype=jnp.int32)[:, None].astype(jnp.float32)
    column_index = jnp.arange(BLOCK, dtype=jnp.int32)[None, :].astype(jnp.float32)
    norm_factor = jnp.sqrt(jnp.where(row_index == 0.0, 1.0, 2.0) / BLOCK).astype(jnp.float32)
    return (norm_factor * jnp.cos(jnp.pi * (2.0 * column_index + 1.0) * row_index / (2.0 * BLOCK))).astype(jnp.float32)

def reference(partials, owner_blocks, momentum, weights, selected):
    gradient = lax.optimization_barrier(jnp.sum(partials, axis=1)) / N_FSDP
    counts = owner_blocks.astype(jnp.int32)
    starts = (jnp.cumsum(counts) - counts).astype(jnp.int32)
    slots = jnp.arange(MOST, dtype=jnp.int32)
    in_use = (slots[None, :] < counts[:, None]).reshape(-1)
    source = jnp.clip(starts[:, None] + slots[None, :], 0, BLOCKS - 1).reshape(-1).astype(jnp.int32)
    gradient_slots = jnp.where(in_use[None, None, :], jnp.take(gradient, source, axis=2), jnp.float32(0.0))
    accumulated = momentum_decay * momentum + gradient_slots
    dct_table = dct_matrix()
    coeffs = jnp.einsum('jv,rvq->rjq', dct_table, accumulated, precision=lax.Precision.HIGHEST)
    picked = jnp.take_along_axis(coeffs, selected, axis=1)
    group_index = jnp.arange(N_REP, dtype=jnp.int32)[:, None, None]
    slot_index = jnp.arange(SLOTS, dtype=jnp.int32)[None, None, :]
    sparse = jnp.zeros(coeffs.shape, jnp.float32).at[group_index, selected, slot_index].set(picked)
    own_part = jnp.einsum('jv,rjq->rvq', dct_table, sparse, precision=lax.Precision.HIGHEST)
    new_momentum = jnp.where(in_use[None, None, :], accumulated - own_part, jnp.float32(0.0))
    combined = lax.optimization_barrier(jnp.sum(sparse, axis=0))
    update = jnp.dot(dct_table.T, combined, precision=lax.Precision.HIGHEST) / N_REP
    new_weights = jnp.where(in_use[None, :], weights - step_rate * update, jnp.float32(0.0))
    return (new_momentum, new_weights)
```

```python
import functools

import jax
import jax.numpy as jnp
import numpy as np
from jax import lax
from jax.experimental import pallas as pl
from jax.experimental.pallas import tpu as pltpu
from jax.sharding import Mesh, PartitionSpec as P

BLOCK = 64
K = 32
BLOCKS = 4096
MOST = 512
OWNERS = 32
GROUPS = 16
NEAR = 8
FAR = OWNERS // NEAR
ROWS = BLOCK // NEAR

REP = ("y", "x")
FSDP = ("zh", "zl", "core")

momentum_decay = 0.9
step_rate = 0.5


def dct_matrix():
    j = np.arange(BLOCK, dtype=np.float64)[:, None]
    v = np.arange(BLOCK, dtype=np.float64)[None, :]
    norm = np.sqrt(np.where(j == 0, 1.0, 2.0) / BLOCK)
    return (norm * np.cos(np.pi * (2 * v + 1) * j / (2 * BLOCK))).astype(np.float32)


def window_kernel(counts_ref, parts_ref, out_ref, total_ref):
    total_ref[:, :BLOCKS] = jnp.sum(parts_ref[...], axis=0)
    total_ref[:, BLOCKS:] = jnp.zeros((ROWS, MOST + 128), jnp.float32)
    lane = lax.broadcasted_iota(jnp.int32, (ROWS, 128), 1)
    start = jnp.int32(0)
    for i in range(OWNERS):
        base = pl.multiple_of((start // 128) * 128, 128)
        shift = start % 128
        tiles = [
            pltpu.roll(total_ref[:, pl.ds(base + 128 * t, 128)], (128 - shift) % 128, 1)
            for t in range(MOST // 128 + 1)
        ]
        for t in range(MOST // 128):
            out_ref[i, :, 128 * t : 128 * (t + 1)] = jnp.where(lane < 128 - shift, tiles[t], tiles[t + 1])
        start = start + counts_ref[i]


def owner_kernel(place_ref, parts_ref, momentum_ref, chosen_ref, table_ref, back_ref, momentum_out_ref, copies_ref):
    count = place_ref[1]
    live = lax.broadcasted_iota(jnp.int32, (BLOCK, MOST), 1) < count
    gradient = jnp.sum(parts_ref[...], axis=0) * (1.0 / OWNERS)
    accumulated = jnp.where(live, momentum_decay * momentum_ref[0] + gradient, 0.0)
    coeffs = jnp.dot(table_ref[...], accumulated, precision=lax.Precision.HIGHEST, preferred_element_type=jnp.float32)
    chosen = chosen_ref[0]
    bit = jnp.left_shift(jnp.int32(1), chosen & 31)
    low = jnp.sum(jnp.where(chosen < 32, bit, 0), axis=0, keepdims=True)
    high = jnp.sum(jnp.where(chosen < 32, 0, bit), axis=0, keepdims=True)
    number = lax.broadcasted_iota(jnp.int32, (32, MOST), 0)
    listed = jnp.concatenate(
        [jnp.right_shift(jnp.broadcast_to(word, (32, MOST)), number) & 1 for word in (low, high)], axis=0
    )
    sparse = jnp.where(listed != 0, coeffs, 0.0)
    own = jnp.dot(back_ref[...], sparse, precision=lax.Precision.HIGHEST, preferred_element_type=jnp.float32)
    momentum_out_ref[0] = jnp.where(live, accumulated - own, 0.0)
    for r in range(GROUPS):
        copies_ref[r] = own


def weights_kernel(place_ref, parts_ref, weights_ref, out_ref):
    live = lax.broadcasted_iota(jnp.int32, (BLOCK, MOST), 1) < place_ref[1]
    update = jnp.sum(parts_ref[...], axis=0) * (1.0 / GROUPS)
    out_ref[...] = jnp.where(live, weights_ref[...] - step_rate * update, 0.0)


def body(partials, owner_blocks, momentum, weights, selected):
    owner = lax.axis_index(FSDP)
    group = lax.axis_index(REP)
    place = jnp.stack([group, owner_blocks[owner]]).astype(jnp.int32)
    whole = pl.BlockSpec(memory_space=pltpu.VMEM)

    near = lax.all_to_all(partials.reshape(NEAR, ROWS, BLOCKS), ("zl", "core"), 0, 0, tiled=False)
    windows = pl.pallas_call(
        window_kernel,
        out_shape=jax.ShapeDtypeStruct((OWNERS, ROWS, MOST), jnp.float32),
        in_specs=[pl.BlockSpec(memory_space=pltpu.SMEM), whole],
        out_specs=whole,
        scratch_shapes=[pltpu.VMEM((ROWS, BLOCKS + MOST + 128), jnp.float32)],
        name="windows",
    )(owner_blocks, near)
    far = lax.all_to_all(windows, FSDP, 0, 0, tiled=False).reshape(FAR, BLOCK, MOST)

    table = dct_matrix()
    new_momentum, copies = pl.pallas_call(
        owner_kernel,
        out_shape=(
            jax.ShapeDtypeStruct((1, BLOCK, MOST), jnp.float32),
            jax.ShapeDtypeStruct((GROUPS, BLOCK, MOST), jnp.float32),
        ),
        grid_spec=pltpu.PrefetchScalarGridSpec(
            num_scalar_prefetch=1,
            grid=(1,),
            in_specs=[
                pl.BlockSpec((FAR, BLOCK, MOST), lambda i, place: (0, 0, 0)),
                pl.BlockSpec((1, BLOCK, MOST), lambda i, place: (0, 0, 0)),
                pl.BlockSpec((1, K, MOST), lambda i, place: (place[0], 0, 0)),
                pl.BlockSpec((BLOCK, BLOCK), lambda i, place: (0, 0)),
                pl.BlockSpec((BLOCK, BLOCK), lambda i, place: (0, 0)),
            ],
            out_specs=[
                pl.BlockSpec((1, BLOCK, MOST), lambda i, place: (0, 0, 0)),
                pl.BlockSpec((GROUPS, BLOCK, MOST), lambda i, place: (0, 0, 0)),
            ],
        ),
        name="owner_step",
    )(place, far, momentum, selected, jnp.asarray(table), jnp.asarray(table.T))
    everyone = lax.all_to_all(copies, REP, 0, 0, tiled=False)
    new_weights = pl.pallas_call(
        weights_kernel,
        out_shape=jax.ShapeDtypeStruct((BLOCK, MOST), jnp.float32),
        in_specs=[pl.BlockSpec(memory_space=pltpu.SMEM), whole, whole],
        out_specs=whole,
        name="weights_step",
    )(place, everyone, weights)
    return new_momentum, new_weights


def solution(mesh):
    fine = Mesh(mesh.devices.reshape(4, 4, FAR, NEAR // 2, 2), REP + FSDP)
    return jax.shard_map(
        body,
        mesh=fine,
        in_specs=(P(REP, FSDP, None, None), P(), P(REP, None, FSDP), P(None, FSDP), P(None, None, FSDP)),
        out_specs=(P(REP, None, FSDP), P(None, FSDP)),
        check_vma=False,
    )
```

```python
import functools

import jax
import jax.numpy as jnp
import numpy as np
from jax import lax
from jax.experimental import pallas as pl
from jax.experimental.pallas import tpu as pltpu
from jax.sharding import Mesh, PartitionSpec as P

BLOCK = 64
K = 32
BLOCKS = 4096
MOST = 512
OWNERS = 32
GROUPS = 16
NEAR = 8
FAR = OWNERS // NEAR
ROWS = BLOCK // NEAR

REP = ("y", "x")
FSDP = ("zh", "zl", "core")

momentum_decay = 0.9
step_rate = 0.5


def dct_matrix():
    j = np.arange(BLOCK, dtype=np.float64)[:, None]
    v = np.arange(BLOCK, dtype=np.float64)[None, :]
    norm = np.sqrt(np.where(j == 0, 1.0, 2.0) / BLOCK)
    return (norm * np.cos(np.pi * (2 * v + 1) * j / (2 * BLOCK))).astype(np.float32)


def window_kernel(place_ref, parts_ref, out_ref, total_ref):
    total_ref[:, :BLOCKS] = jnp.sum(parts_ref[...], axis=0)
    total_ref[:, BLOCKS:] = jnp.zeros((ROWS, MOST + 128), jnp.float32)
    lane = lax.broadcasted_iota(jnp.int32, (ROWS, 128), 1)
    start = jnp.int32(0)
    for i in range(OWNERS):
        base = pl.multiple_of((start // 128) * 128, 128)
        shift = start % 128
        tiles = [
            pltpu.roll(total_ref[:, pl.ds(base + 128 * t, 128)], (128 - shift) % 128, 1)
            for t in range(MOST // 128 + 1)
        ]
        for t in range(MOST // 128):
            out_ref[i, :, 128 * t : 128 * (t + 1)] = jnp.where(lane < 128 - shift, tiles[t], tiles[t + 1])
        start = start + place_ref[2 + i]


def owner_kernel(place_ref, parts_ref, momentum_ref, chosen_ref, table_ref, back_ref, momentum_out_ref, copies_ref):
    count = place_ref[1]
    live = lax.broadcasted_iota(jnp.int32, (BLOCK, MOST), 1) < count
    gradient = jnp.sum(parts_ref[...], axis=0) * (1.0 / OWNERS)
    accumulated = jnp.where(live, momentum_decay * momentum_ref[0] + gradient, 0.0)
    coeffs = jnp.dot(table_ref[...], accumulated, precision=lax.Precision.HIGHEST, preferred_element_type=jnp.float32)
    chosen = chosen_ref[0]
    bit = jnp.left_shift(jnp.int32(1), chosen & 31)
    low = jnp.sum(jnp.where(chosen < 32, bit, 0), axis=0, keepdims=True)
    high = jnp.sum(jnp.where(chosen < 32, 0, bit), axis=0, keepdims=True)
    number = lax.broadcasted_iota(jnp.int32, (32, MOST), 0)
    listed = jnp.concatenate(
        [jnp.right_shift(jnp.broadcast_to(word, (32, MOST)), number) & 1 for word in (low, high)], axis=0
    )
    sparse = jnp.where(listed != 0, coeffs, 0.0)
    own = jnp.dot(back_ref[...], sparse, precision=lax.Precision.HIGHEST, preferred_element_type=jnp.float32)
    momentum_out_ref[0] = jnp.where(live, accumulated - own, 0.0)
    for r in range(GROUPS):
        copies_ref[r] = own


def weights_kernel(place_ref, parts_ref, weights_ref, out_ref):
    live = lax.broadcasted_iota(jnp.int32, (BLOCK, MOST), 1) < place_ref[1]
    update = jnp.sum(parts_ref[...], axis=0) * (1.0 / GROUPS)
    out_ref[...] = jnp.where(live, weights_ref[...] - step_rate * update, 0.0)


def body(partials, owner_blocks, momentum, weights, selected):
    owner = lax.axis_index(FSDP)
    group = lax.axis_index(REP)
    place = jnp.concatenate([jnp.stack([group, owner_blocks[owner]]).astype(jnp.int32), owner_blocks])
    whole = pl.BlockSpec(memory_space=pltpu.VMEM)

    near = lax.all_to_all(partials.reshape(NEAR, ROWS, BLOCKS), ("zl", "core"), 0, 0, tiled=False)
    windows = pl.pallas_call(
        window_kernel,
        out_shape=jax.ShapeDtypeStruct((OWNERS, ROWS, MOST), jnp.float32),
        in_specs=[pl.BlockSpec(memory_space=pltpu.SMEM), whole],
        out_specs=whole,
        scratch_shapes=[pltpu.VMEM((ROWS, BLOCKS + MOST + 128), jnp.float32)],
        compiler_params=pltpu.CompilerParams(vmem_limit_bytes=8 << 20),
        name="windows",
    )(place, near)
    far = lax.all_to_all(windows, FSDP, 0, 0, tiled=False).reshape(FAR, BLOCK, MOST)

    table = dct_matrix()
    new_momentum, copies = pl.pallas_call(
        owner_kernel,
        out_shape=(
            jax.ShapeDtypeStruct((1, BLOCK, MOST), jnp.float32),
            jax.ShapeDtypeStruct((GROUPS, BLOCK, MOST), jnp.float32),
        ),
        grid_spec=pltpu.PrefetchScalarGridSpec(
            num_scalar_prefetch=1,
            grid=(1,),
            in_specs=[
                pl.BlockSpec((FAR, BLOCK, MOST), lambda i, place: (0, 0, 0)),
                pl.BlockSpec((1, BLOCK, MOST), lambda i, place: (0, 0, 0)),
                pl.BlockSpec((1, K, MOST), lambda i, place: (place[0], 0, 0)),
                pl.BlockSpec((BLOCK, BLOCK), lambda i, place: (0, 0)),
                pl.BlockSpec((BLOCK, BLOCK), lambda i, place: (0, 0)),
            ],
            out_specs=[
                pl.BlockSpec((1, BLOCK, MOST), lambda i, place: (0, 0, 0)),
                pl.BlockSpec((GROUPS, BLOCK, MOST), lambda i, place: (0, 0, 0)),
            ],
        ),
        compiler_params=pltpu.CompilerParams(vmem_limit_bytes=16 << 20),
        name="owner_step",
    )(place, far, momentum, selected, jnp.asarray(table), jnp.asarray(table.T))
    everyone = lax.all_to_all(copies, REP, 0, 0, tiled=False)
    new_weights = pl.pallas_call(
        weights_kernel,
        out_shape=jax.ShapeDtypeStruct((BLOCK, MOST), jnp.float32),
        in_specs=[pl.BlockSpec(memory_space=pltpu.SMEM), whole, whole],
        out_specs=whole,
        compiler_params=pltpu.CompilerParams(vmem_limit_bytes=8 << 20),
        name="weights_step",
    )(place, everyone, weights)
    return new_momentum, new_weights


def solution(mesh):
    fine = Mesh(mesh.devices.reshape(4, 4, FAR, NEAR // 2, 2), REP + FSDP)
    return jax.shard_map(
        body,
        mesh=fine,
        in_specs=(P(REP, FSDP, None, None), P(), P(REP, None, FSDP), P(None, FSDP), P(None, None, FSDP)),
        out_specs=(P(REP, None, FSDP), P(None, FSDP)),
        check_vma=False,
    )
```

```python
import functools

import jax
import jax.numpy as jnp
import numpy as np
from jax import lax
from jax.experimental import pallas as pl
from jax.experimental.pallas import tpu as pltpu
from jax.sharding import Mesh, PartitionSpec as P

BLOCK = 64
K = 32
BLOCKS = 4096
MOST = 512
OWNERS = 32
GROUPS = 16
NEAR = 8
CHIPS = NEAR // 2
SIDE = 4
FAR = OWNERS // NEAR
ROWS = BLOCK // NEAR

REP = ("y", "x")
FSDP = ("zh", "zl", "core")

momentum_decay = 0.9
step_rate = 0.5


def dct_matrix():
    j = np.arange(BLOCK, dtype=np.float64)[:, None]
    v = np.arange(BLOCK, dtype=np.float64)[None, :]
    norm = np.sqrt(np.where(j == 0, 1.0, 2.0) / BLOCK)
    return (norm * np.cos(np.pi * (2 * v + 1) * j / (2 * BLOCK))).astype(np.float32)


def add_cores_kernel(parts_ref, out_ref):
    out_ref[...] = parts_ref[0] + parts_ref[1]


def window_kernel(place_ref, parts_ref, out_ref, total_ref):
    total_ref[:, :BLOCKS] = jnp.sum(parts_ref[...], axis=0)
    total_ref[:, BLOCKS:] = jnp.zeros((ROWS, MOST + 128), jnp.float32)
    lane = lax.broadcasted_iota(jnp.int32, (ROWS, 128), 1)
    start = jnp.int32(0)
    for i in range(OWNERS):
        base = pl.multiple_of((start // 128) * 128, 128)
        shift = start % 128
        tiles = [
            pltpu.roll(total_ref[:, pl.ds(base + 128 * t, 128)], (128 - shift) % 128, 1)
            for t in range(MOST // 128 + 1)
        ]
        for t in range(MOST // 128):
            out_ref[i, :, 128 * t : 128 * (t + 1)] = jnp.where(lane < 128 - shift, tiles[t], tiles[t + 1])
        start = start + place_ref[2 + i]


def owner_kernel(place_ref, parts_ref, momentum_ref, chosen_ref, table_ref, back_ref, momentum_out_ref, copies_ref):
    count = place_ref[1]
    live = lax.broadcasted_iota(jnp.int32, (BLOCK, MOST), 1) < count
    added = jnp.sum(parts_ref[...], axis=0)
    gradient = jnp.concatenate([added[b, c] for c in range(2) for b in range(CHIPS)], axis=0) * (1.0 / OWNERS)
    accumulated = jnp.where(live, momentum_decay * momentum_ref[0] + gradient, 0.0)
    coeffs = jnp.dot(table_ref[...], accumulated, precision=lax.Precision.HIGHEST, preferred_element_type=jnp.float32)
    chosen = chosen_ref[0]
    bit = jnp.left_shift(jnp.int32(1), chosen & 31)
    low = jnp.sum(jnp.where(chosen < 32, bit, 0), axis=0, keepdims=True)
    high = jnp.sum(jnp.where(chosen < 32, 0, bit), axis=0, keepdims=True)
    number = lax.broadcasted_iota(jnp.int32, (32, MOST), 0)
    listed = jnp.concatenate(
        [jnp.right_shift(jnp.broadcast_to(word, (32, MOST)), number) & 1 for word in (low, high)], axis=0
    )
    sparse = jnp.where(listed != 0, coeffs, 0.0)
    own = jnp.dot(back_ref[...], sparse, precision=lax.Precision.HIGHEST, preferred_element_type=jnp.float32)
    momentum_out_ref[0] = jnp.where(live, accumulated - own, 0.0)
    for r in range(SIDE):
        copies_ref[r] = own


def add_row_kernel(parts_ref, copies_ref):
    added = jnp.sum(parts_ref[...], axis=0)
    for r in range(SIDE):
        copies_ref[r] = added


def weights_kernel(place_ref, parts_ref, weights_ref, out_ref):
    live = lax.broadcasted_iota(jnp.int32, (BLOCK, MOST), 1) < place_ref[1]
    update = jnp.sum(parts_ref[...], axis=0) * (1.0 / GROUPS)
    out_ref[...] = jnp.where(live, weights_ref[...] - step_rate * update, 0.0)


def body(partials, owner_blocks, momentum, weights, selected):
    owner = lax.axis_index(FSDP)
    group = lax.axis_index(REP)
    place = jnp.concatenate([jnp.stack([group, owner_blocks[owner]]).astype(jnp.int32), owner_blocks])
    whole = pl.BlockSpec(memory_space=pltpu.VMEM)

    halves = lax.all_to_all(partials.reshape(2, BLOCK // 2, BLOCKS), "core", 0, 0, tiled=False)
    half = pl.pallas_call(
        add_cores_kernel,
        out_shape=jax.ShapeDtypeStruct((BLOCK // 2, BLOCKS), jnp.float32),
        in_specs=[whole],
        out_specs=whole,
        compiler_params=pltpu.CompilerParams(vmem_limit_bytes=8 << 20),
        name="add_cores",
    )(halves)
    near = lax.all_to_all(half.reshape(CHIPS, ROWS, BLOCKS), "zl", 0, 0, tiled=False)
    windows = pl.pallas_call(
        window_kernel,
        out_shape=jax.ShapeDtypeStruct((OWNERS, ROWS, MOST), jnp.float32),
        in_specs=[pl.BlockSpec(memory_space=pltpu.SMEM), whole],
        out_specs=whole,
        scratch_shapes=[pltpu.VMEM((ROWS, BLOCKS + MOST + 128), jnp.float32)],
        compiler_params=pltpu.CompilerParams(vmem_limit_bytes=8 << 20),
        name="windows",
    )(place, near)
    far = lax.all_to_all(windows, FSDP, 0, 0, tiled=False).reshape(FAR, CHIPS, 2, ROWS, MOST)

    table = dct_matrix()
    new_momentum, copies = pl.pallas_call(
        owner_kernel,
        out_shape=(
            jax.ShapeDtypeStruct((1, BLOCK, MOST), jnp.float32),
            jax.ShapeDtypeStruct((SIDE, BLOCK, MOST), jnp.float32),
        ),
        grid_spec=pltpu.PrefetchScalarGridSpec(
            num_scalar_prefetch=1,
            grid=(1,),
            in_specs=[
                pl.BlockSpec((FAR, CHIPS, 2, ROWS, MOST), lambda i, place: (0, 0, 0, 0, 0)),
                pl.BlockSpec((1, BLOCK, MOST), lambda i, place: (0, 0, 0)),
                pl.BlockSpec((1, K, MOST), lambda i, place: (place[0], 0, 0)),
                pl.BlockSpec((BLOCK, BLOCK), lambda i, place: (0, 0)),
                pl.BlockSpec((BLOCK, BLOCK), lambda i, place: (0, 0)),
            ],
            out_specs=[
                pl.BlockSpec((1, BLOCK, MOST), lambda i, place: (0, 0, 0)),
                pl.BlockSpec((SIDE, BLOCK, MOST), lambda i, place: (0, 0, 0)),
            ],
        ),
        compiler_params=pltpu.CompilerParams(vmem_limit_bytes=16 << 20),
        name="owner_step",
    )(place, far, momentum, selected, jnp.asarray(table), jnp.asarray(table.T))
    row = lax.all_to_all(copies, "x", 0, 0, tiled=False)
    copies = pl.pallas_call(
        add_row_kernel,
        out_shape=jax.ShapeDtypeStruct((SIDE, BLOCK, MOST), jnp.float32),
        in_specs=[whole],
        out_specs=whole,
        compiler_params=pltpu.CompilerParams(vmem_limit_bytes=8 << 20),
        name="add_row",
    )(row)
    everyone = lax.all_to_all(copies, "y", 0, 0, tiled=False)
    new_weights = pl.pallas_call(
        weights_kernel,
        out_shape=jax.ShapeDtypeStruct((BLOCK, MOST), jnp.float32),
        in_specs=[pl.BlockSpec(memory_space=pltpu.SMEM), whole, whole],
        out_specs=whole,
        compiler_params=pltpu.CompilerParams(vmem_limit_bytes=8 << 20),
        name="weights_step",
    )(place, everyone, weights)
    return new_momentum, new_weights


def solution(mesh):
    fine = Mesh(mesh.devices.reshape(SIDE, SIDE, FAR, CHIPS, 2), REP + FSDP)
    return jax.shard_map(
        body,
        mesh=fine,
        in_specs=(P(REP, FSDP, None, None), P(), P(REP, None, FSDP), P(None, FSDP), P(None, None, FSDP)),
        out_specs=(P(REP, None, FSDP), P(None, FSDP)),
        check_vma=False,
    )
```

```python
import functools

import jax
import jax.numpy as jnp
import numpy as np
from jax import lax
from jax.experimental import pallas as pl
from jax.experimental.pallas import tpu as pltpu
from jax.sharding import Mesh, PartitionSpec as P

BLOCK = 64
K = 32
BLOCKS = 4096
MOST = 512
OWNERS = 32
GROUPS = 16
NEAR = 8
CHIPS = NEAR // 2
SIDE = 4
WIDTHS = (1536, 2048, 4096)
FAR = OWNERS // NEAR
ROWS = BLOCK // NEAR

REP = ("y", "x")
FSDP = ("zh", "zl", "core")

momentum_decay = 0.9
step_rate = 0.5


def dct_matrix():
    j = np.arange(BLOCK, dtype=np.float64)[:, None]
    v = np.arange(BLOCK, dtype=np.float64)[None, :]
    norm = np.sqrt(np.where(j == 0, 1.0, 2.0) / BLOCK)
    return (norm * np.cos(np.pi * (2 * v + 1) * j / (2 * BLOCK))).astype(np.float32)


def add_cores_kernel(parts_ref, out_ref):
    out_ref[...] = parts_ref[0] + parts_ref[1]


def plan_kernel(where_ref, counts_ref, plan_ref):
    plan_ref[0] = where_ref[0]
    plan_ref[1] = counts_ref[where_ref[1]]
    start = jnp.int32(0)
    reach = jnp.int32(0)
    first = jnp.int32(0)
    for i in range(OWNERS):
        if i % NEAR == 0:
            first = start - start % 128
        plan_ref[3 + i] = start
        start = start + counts_ref[i]
        reach = jnp.maximum(reach, start - first)
    plan_ref[2] = sum((reach > width).astype(jnp.int32) for width in WIDTHS[:-1])


def spread_kernel(width, plan_ref, parts_ref, out_ref, total_ref):
    total_ref[:, :BLOCKS] = jnp.sum(parts_ref[...], axis=0)
    total_ref[:, BLOCKS:] = jnp.zeros((ROWS, width), jnp.float32)
    for a in range(FAR):
        base = pl.multiple_of((plan_ref[3 + NEAR * a] // 128) * 128, 128)
        out_ref[a] = total_ref[:, pl.ds(base, width)]


def window_kernel(width, plan_ref, far_ref, parts_ref, out_ref, total_ref):
    total_ref[:, :width] = jnp.sum(parts_ref[...], axis=0)
    total_ref[:, width:] = jnp.zeros((ROWS, MOST + 128), jnp.float32)
    lane = lax.broadcasted_iota(jnp.int32, (ROWS, 128), 1)
    owner = far_ref[0] * NEAR
    first = (plan_ref[3 + owner] // 128) * 128
    for i in range(NEAR):
        start = plan_ref[3 + owner + i] - first
        base = pl.multiple_of((start // 128) * 128, 128)
        shift = start % 128
        tiles = [
            pltpu.roll(total_ref[:, pl.ds(base + 128 * t, 128)], (128 - shift) % 128, 1)
            for t in range(MOST // 128 + 1)
        ]
        for t in range(MOST // 128):
            out_ref[i, :, 128 * t : 128 * (t + 1)] = jnp.where(lane < 128 - shift, tiles[t], tiles[t + 1])


def deliver(width, plan, far, near):
    smem = pl.BlockSpec(memory_space=pltpu.SMEM)
    whole = pl.BlockSpec(memory_space=pltpu.VMEM)
    small = pltpu.CompilerParams(vmem_limit_bytes=8 << 20)
    spread = pl.pallas_call(
        functools.partial(spread_kernel, width),
        out_shape=jax.ShapeDtypeStruct((FAR, ROWS, width), jnp.float32),
        in_specs=[smem, whole],
        out_specs=whole,
        scratch_shapes=[pltpu.VMEM((ROWS, BLOCKS + width), jnp.float32)],
        compiler_params=small,
        name=f"spread_{width}",
    )(plan, near)
    met = lax.all_to_all(spread, "zh", 0, 0, tiled=False)
    return pl.pallas_call(
        functools.partial(window_kernel, width),
        out_shape=jax.ShapeDtypeStruct((NEAR, ROWS, MOST), jnp.float32),
        in_specs=[smem, smem, whole],
        out_specs=whole,
        scratch_shapes=[pltpu.VMEM((ROWS, width + MOST + 128), jnp.float32)],
        compiler_params=small,
        name=f"windows_{width}",
    )(plan, far, met)


def owner_kernel(place_ref, parts_ref, momentum_ref, chosen_ref, table_ref, back_ref, momentum_out_ref, copies_ref):
    count = place_ref[1]
    live = lax.broadcasted_iota(jnp.int32, (BLOCK, MOST), 1) < count
    gradient = jnp.concatenate([parts_ref[b, c] for c in range(2) for b in range(CHIPS)], axis=0) * (1.0 / OWNERS)
    accumulated = jnp.where(live, momentum_decay * momentum_ref[0] + gradient, 0.0)
    coeffs = jnp.dot(table_ref[...], accumulated, precision=lax.Precision.HIGHEST, preferred_element_type=jnp.float32)
    chosen = chosen_ref[0]
    bit = jnp.left_shift(jnp.int32(1), chosen & 31)
    low = jnp.sum(jnp.where(chosen < 32, bit, 0), axis=0, keepdims=True)
    high = jnp.sum(jnp.where(chosen < 32, 0, bit), axis=0, keepdims=True)
    number = lax.broadcasted_iota(jnp.int32, (32, MOST), 0)
    listed = jnp.concatenate(
        [jnp.right_shift(jnp.broadcast_to(word, (32, MOST)), number) & 1 for word in (low, high)], axis=0
    )
    sparse = jnp.where(listed != 0, coeffs, 0.0)
    own = jnp.dot(back_ref[...], sparse, precision=lax.Precision.HIGHEST, preferred_element_type=jnp.float32)
    momentum_out_ref[0] = jnp.where(live, accumulated - own, 0.0)
    for r in range(SIDE):
        copies_ref[r] = own


def add_row_kernel(parts_ref, copies_ref):
    added = jnp.sum(parts_ref[...], axis=0)
    for r in range(SIDE):
        copies_ref[r] = added


def weights_kernel(place_ref, parts_ref, weights_ref, out_ref):
    live = lax.broadcasted_iota(jnp.int32, (BLOCK, MOST), 1) < place_ref[1]
    update = jnp.sum(parts_ref[...], axis=0) * (1.0 / GROUPS)
    out_ref[...] = jnp.where(live, weights_ref[...] - step_rate * update, 0.0)


def body(partials, owner_blocks, momentum, weights, selected):
    owner = lax.axis_index(FSDP)
    group = lax.axis_index(REP)
    far = lax.axis_index("zh").reshape(1)
    smem = pl.BlockSpec(memory_space=pltpu.SMEM)
    place = pl.pallas_call(
        plan_kernel,
        out_shape=jax.ShapeDtypeStruct((3 + OWNERS,), jnp.int32),
        in_specs=[smem, smem],
        out_specs=smem,
        name="plan",
    )(jnp.stack([group, owner]).astype(jnp.int32), owner_blocks)
    whole = pl.BlockSpec(memory_space=pltpu.VMEM)

    halves = lax.all_to_all(partials.reshape(2, BLOCK // 2, BLOCKS), "core", 0, 0, tiled=False)
    half = pl.pallas_call(
        add_cores_kernel,
        out_shape=jax.ShapeDtypeStruct((BLOCK // 2, BLOCKS), jnp.float32),
        in_specs=[whole],
        out_specs=whole,
        compiler_params=pltpu.CompilerParams(vmem_limit_bytes=8 << 20),
        name="add_cores",
    )(halves)
    near = lax.all_to_all(half.reshape(CHIPS, ROWS, BLOCKS), "zl", 0, 0, tiled=False)
    windows = lax.switch(place[2], [functools.partial(deliver, width) for width in WIDTHS], place, far, near)
    blocks = lax.all_to_all(windows, ("zl", "core"), 0, 0, tiled=False).reshape(CHIPS, 2, ROWS, MOST)

    table = dct_matrix()
    new_momentum, copies = pl.pallas_call(
        owner_kernel,
        out_shape=(
            jax.ShapeDtypeStruct((1, BLOCK, MOST), jnp.float32),
            jax.ShapeDtypeStruct((SIDE, BLOCK, MOST), jnp.float32),
        ),
        grid_spec=pltpu.PrefetchScalarGridSpec(
            num_scalar_prefetch=1,
            grid=(1,),
            in_specs=[
                pl.BlockSpec((CHIPS, 2, ROWS, MOST), lambda i, place: (0, 0, 0, 0)),
                pl.BlockSpec((1, BLOCK, MOST), lambda i, place: (0, 0, 0)),
                pl.BlockSpec((1, K, MOST), lambda i, place: (place[0], 0, 0)),
                pl.BlockSpec((BLOCK, BLOCK), lambda i, place: (0, 0)),
                pl.BlockSpec((BLOCK, BLOCK), lambda i, place: (0, 0)),
            ],
            out_specs=[
                pl.BlockSpec((1, BLOCK, MOST), lambda i, place: (0, 0, 0)),
                pl.BlockSpec((SIDE, BLOCK, MOST), lambda i, place: (0, 0, 0)),
            ],
        ),
        compiler_params=pltpu.CompilerParams(vmem_limit_bytes=16 << 20),
        name="owner_step",
    )(place, blocks, momentum, selected, jnp.asarray(table), jnp.asarray(table.T))
    row = lax.all_to_all(copies, "x", 0, 0, tiled=False)
    copies = pl.pallas_call(
        add_row_kernel,
        out_shape=jax.ShapeDtypeStruct((SIDE, BLOCK, MOST), jnp.float32),
        in_specs=[whole],
        out_specs=whole,
        compiler_params=pltpu.CompilerParams(vmem_limit_bytes=8 << 20),
        name="add_row",
    )(row)
    everyone = lax.all_to_all(copies, "y", 0, 0, tiled=False)
    new_weights = pl.pallas_call(
        weights_kernel,
        out_shape=jax.ShapeDtypeStruct((BLOCK, MOST), jnp.float32),
        in_specs=[pl.BlockSpec(memory_space=pltpu.SMEM), whole, whole],
        out_specs=whole,
        compiler_params=pltpu.CompilerParams(vmem_limit_bytes=8 << 20),
        name="weights_step",
    )(place, everyone, weights)
    return new_momentum, new_weights


def solution(mesh):
    fine = Mesh(mesh.devices.reshape(SIDE, SIDE, FAR, CHIPS, 2), REP + FSDP)
    return jax.shard_map(
        body,
        mesh=fine,
        in_specs=(P(REP, FSDP, None, None), P(), P(REP, None, FSDP), P(None, FSDP), P(None, None, FSDP)),
        out_specs=(P(REP, None, FSDP), P(None, FSDP)),
        check_vma=False,
    )
```

```python
import functools

import jax
import jax.numpy as jnp
import numpy as np
from jax import lax
from jax.experimental import pallas as pl
from jax.experimental.pallas import tpu as pltpu
from jax.sharding import Mesh, PartitionSpec as P

BLOCK = 64
K = 32
BLOCKS = 4096
MOST = 512
OWNERS = 32
GROUPS = 16
NEAR = 8
CHIPS = NEAR // 2
SIDE = 4
WIDTHS = (1536, 2048, 4096)
FAR = OWNERS // NEAR
ROWS = BLOCK // NEAR

REP = ("y", "x")
FSDP = ("zh", "zl", "core")

momentum_decay = 0.9
step_rate = 0.5


def dct_matrix():
    j = np.arange(BLOCK, dtype=np.float64)[:, None]
    v = np.arange(BLOCK, dtype=np.float64)[None, :]
    norm = np.sqrt(np.where(j == 0, 1.0, 2.0) / BLOCK)
    return (norm * np.cos(np.pi * (2 * v + 1) * j / (2 * BLOCK))).astype(np.float32)


def near_groups():
    return [
        [(CHIPS * a + b + 2 * core) % (OWNERS // 2) * 2 + core for b in range(CHIPS)]
        for a in range(FAR)
        for core in range(2)
    ]


def rep_groups(turn):
    groups = []
    for core in range(2):
        for z in range(OWNERS // 2):
            for i in range(SIDE):
                line = [(i * SIDE + k if core == turn else k * SIDE + i) for k in range(SIDE)]
                groups.append([rep * OWNERS + 2 * z + core for rep in line])
    return groups


def add_cores_kernel(plan_ref, parts_ref, out_ref):
    del plan_ref
    out_ref[...] = parts_ref[0] + parts_ref[1]


def plan_kernel(where_ref, counts_ref, plan_ref, branch_ref):
    plan_ref[0] = where_ref[0]
    plan_ref[1] = counts_ref[where_ref[1]]
    start = jnp.int32(0)
    reach = jnp.int32(0)
    first = jnp.int32(0)
    for i in range(OWNERS):
        if i % NEAR == 0:
            first = start - start % 128
        plan_ref[2 + i] = start
        start = start + counts_ref[i]
        reach = jnp.maximum(reach, start - first)
    branch_ref[0] = sum((reach > width).astype(jnp.int32) for width in WIDTHS[:-1])


def spread_kernel(width, plan_ref, parts_ref, out_ref, total_ref):
    total_ref[:, :BLOCKS] = jnp.sum(parts_ref[...], axis=0)
    total_ref[:, BLOCKS:] = jnp.zeros((ROWS, width), jnp.float32)
    for a in range(FAR):
        base = pl.multiple_of((plan_ref[2 + NEAR * a] // 128) * 128, 128)
        out_ref[a] = total_ref[:, pl.ds(base, width)]


def window_kernel(width, plan_ref, far_ref, parts_ref, out_ref, total_ref):
    total_ref[:, :width] = jnp.sum(parts_ref[...], axis=0)
    total_ref[:, width:] = jnp.zeros((ROWS, MOST + 128), jnp.float32)
    lane = lax.broadcasted_iota(jnp.int32, (ROWS, 128), 1)
    owner = far_ref[0] * NEAR
    first = (plan_ref[2 + owner] // 128) * 128
    for i in range(NEAR):
        start = plan_ref[2 + owner + i] - first
        base = pl.multiple_of((start // 128) * 128, 128)
        shift = start % 128
        tiles = [
            pltpu.roll(total_ref[:, pl.ds(base + 128 * t, 128)], (128 - shift) % 128, 1)
            for t in range(MOST // 128 + 1)
        ]
        for t in range(MOST // 128):
            out_ref[i, :, 128 * t : 128 * (t + 1)] = jnp.where(lane < 128 - shift, tiles[t], tiles[t + 1])


def deliver(width, plan, far, near):
    smem = pl.BlockSpec(memory_space=pltpu.SMEM)
    whole = pl.BlockSpec(memory_space=pltpu.VMEM)
    small = pltpu.CompilerParams(vmem_limit_bytes=8 << 20)
    spread = pl.pallas_call(
        functools.partial(spread_kernel, width),
        out_shape=jax.ShapeDtypeStruct((FAR, ROWS, width), jnp.float32),
        in_specs=[smem, whole],
        out_specs=whole,
        scratch_shapes=[pltpu.VMEM((ROWS, BLOCKS + width), jnp.float32)],
        compiler_params=small,
        name=f"spread_{width}",
    )(plan, near)
    met = lax.all_to_all(spread, "zh", 0, 0, tiled=False)
    return pl.pallas_call(
        functools.partial(window_kernel, width),
        out_shape=jax.ShapeDtypeStruct((NEAR, ROWS, MOST), jnp.float32),
        in_specs=[smem, smem, whole],
        out_specs=whole,
        scratch_shapes=[pltpu.VMEM((ROWS, width + MOST + 128), jnp.float32)],
        compiler_params=small,
        name=f"windows_{width}",
    )(plan, far, met)


def owner_kernel(place_ref, parts_ref, momentum_ref, chosen_ref, table_ref, back_ref, momentum_out_ref, copies_ref):
    count = place_ref[1]
    live = lax.broadcasted_iota(jnp.int32, (BLOCK, MOST), 1) < count
    gradient = jnp.concatenate([parts_ref[(b + 2 * c) % CHIPS, c] for c in range(2) for b in range(CHIPS)], axis=0) * (1.0 / OWNERS)
    accumulated = jnp.where(live, momentum_decay * momentum_ref[0] + gradient, 0.0)
    coeffs = jnp.dot(table_ref[...], accumulated, precision=lax.Precision.HIGHEST, preferred_element_type=jnp.float32)
    chosen = chosen_ref[0]
    bit = jnp.left_shift(jnp.int32(1), chosen & 31)
    low = jnp.sum(jnp.where(chosen < 32, bit, 0), axis=0, keepdims=True)
    high = jnp.sum(jnp.where(chosen < 32, 0, bit), axis=0, keepdims=True)
    number = lax.broadcasted_iota(jnp.int32, (32, MOST), 0)
    listed = jnp.concatenate(
        [jnp.right_shift(jnp.broadcast_to(word, (32, MOST)), number) & 1 for word in (low, high)], axis=0
    )
    sparse = jnp.where(listed != 0, coeffs, 0.0)
    own = jnp.dot(back_ref[...], sparse, precision=lax.Precision.HIGHEST, preferred_element_type=jnp.float32)
    momentum_out_ref[0] = jnp.where(live, accumulated - own, 0.0)
    for r in range(SIDE):
        copies_ref[r] = own


def add_row_kernel(parts_ref, copies_ref):
    added = jnp.sum(parts_ref[...], axis=0)
    for r in range(SIDE):
        copies_ref[r] = added


def weights_kernel(place_ref, parts_ref, weights_ref, out_ref):
    live = lax.broadcasted_iota(jnp.int32, (BLOCK, MOST), 1) < place_ref[1]
    update = jnp.sum(parts_ref[...], axis=0) * (1.0 / GROUPS)
    out_ref[...] = jnp.where(live, weights_ref[...] - step_rate * update, 0.0)


def body(partials, owner_blocks, momentum, weights, selected):
    owner = lax.axis_index(FSDP)
    group = lax.axis_index(REP)
    far = lax.axis_index("zh").reshape(1)
    smem = pl.BlockSpec(memory_space=pltpu.SMEM)
    place, branch = pl.pallas_call(
        plan_kernel,
        out_shape=(jax.ShapeDtypeStruct((2 + OWNERS,), jnp.int32), jax.ShapeDtypeStruct((1,), jnp.int32)),
        in_specs=[smem, smem],
        out_specs=(smem, smem),
        compiler_params=pltpu.CompilerParams(vmem_limit_bytes=1 << 20),
        name="plan",
    )(jnp.stack([group, owner]).astype(jnp.int32), owner_blocks)
    whole = pl.BlockSpec(memory_space=pltpu.VMEM)

    halves = lax.all_to_all(partials.reshape(2, BLOCK // 2, BLOCKS), "core", 0, 0, tiled=False)
    half = pl.pallas_call(
        add_cores_kernel,
        out_shape=jax.ShapeDtypeStruct((BLOCK // 2, BLOCKS), jnp.float32),
        in_specs=[pl.BlockSpec(memory_space=pl.ANY), whole],
        out_specs=whole,
        compiler_params=pltpu.CompilerParams(vmem_limit_bytes=8 << 20),
        name="add_cores",
    )(place, halves)
    near = lax.all_to_all(half.reshape(CHIPS, ROWS, BLOCKS), FSDP, 0, 0, axis_index_groups=near_groups(), tiled=False)
    windows = lax.switch(branch[0], [functools.partial(deliver, width) for width in WIDTHS], place, far, near)
    blocks = lax.all_to_all(windows, ("zl", "core"), 0, 0, tiled=False).reshape(CHIPS, 2, ROWS, MOST)

    table = dct_matrix()
    new_momentum, copies = pl.pallas_call(
        owner_kernel,
        out_shape=(
            jax.ShapeDtypeStruct((1, BLOCK, MOST), jnp.float32),
            jax.ShapeDtypeStruct((SIDE, BLOCK, MOST), jnp.float32),
        ),
        grid_spec=pltpu.PrefetchScalarGridSpec(
            num_scalar_prefetch=1,
            grid=(1,),
            in_specs=[
                pl.BlockSpec((CHIPS, 2, ROWS, MOST), lambda i, place: (0, 0, 0, 0)),
                pl.BlockSpec((1, BLOCK, MOST), lambda i, place: (0, 0, 0)),
                pl.BlockSpec((1, K, MOST), lambda i, place: (place[0], 0, 0)),
                pl.BlockSpec((BLOCK, BLOCK), lambda i, place: (0, 0)),
                pl.BlockSpec((BLOCK, BLOCK), lambda i, place: (0, 0)),
            ],
            out_specs=[
                pl.BlockSpec((1, BLOCK, MOST), lambda i, place: (0, 0, 0)),
                pl.BlockSpec((SIDE, BLOCK, MOST), lambda i, place: (0, 0, 0)),
            ],
        ),
        compiler_params=pltpu.CompilerParams(vmem_limit_bytes=16 << 20),
        name="owner_step",
    )(place, blocks, momentum, selected, jnp.asarray(table), jnp.asarray(table.T))
    row = lax.all_to_all(copies, REP + FSDP, 0, 0, axis_index_groups=rep_groups(0), tiled=False)
    copies = pl.pallas_call(
        add_row_kernel,
        out_shape=jax.ShapeDtypeStruct((SIDE, BLOCK, MOST), jnp.float32),
        in_specs=[whole],
        out_specs=whole,
        compiler_params=pltpu.CompilerParams(vmem_limit_bytes=8 << 20),
        name="add_row",
    )(row)
    everyone = lax.all_to_all(copies, REP + FSDP, 0, 0, axis_index_groups=rep_groups(1), tiled=False)
    new_weights = pl.pallas_call(
        weights_kernel,
        out_shape=jax.ShapeDtypeStruct((BLOCK, MOST), jnp.float32),
        in_specs=[pl.BlockSpec(memory_space=pltpu.SMEM), whole, whole],
        out_specs=whole,
        compiler_params=pltpu.CompilerParams(vmem_limit_bytes=8 << 20),
        name="weights_step",
    )(place, everyone, weights)
    return new_momentum, new_weights


def solution(mesh):
    fine = Mesh(mesh.devices.reshape(SIDE, SIDE, FAR, CHIPS, 2), REP + FSDP)
    return jax.shard_map(
        body,
        mesh=fine,
        in_specs=(P(REP, FSDP, None, None), P(), P(REP, None, FSDP), P(None, FSDP), P(None, None, FSDP)),
        out_specs=(P(REP, None, FSDP), P(None, FSDP)),
        check_vma=False,
    )
```

```python
import functools

import jax
import jax.numpy as jnp
import numpy as np
from jax import lax
from jax.experimental import pallas as pl
from jax.experimental.pallas import tpu as pltpu
from jax.sharding import Mesh, PartitionSpec as P

BLOCK = 64
K = 32
BLOCKS = 4096
MOST = 512
OWNERS = 32
GROUPS = 16
NEAR = 8
CHIPS = NEAR // 2
SIDE = 4
WIDTHS = (1280, 1408, 1536, 1664, 1792, 2048, 2560, 4096)
FAR = OWNERS // NEAR
ROWS = BLOCK // NEAR

REP = ("y", "x")
FSDP = ("zh", "zl", "core")

momentum_decay = 0.9
step_rate = 0.5


def dct_matrix():
    j = np.arange(BLOCK, dtype=np.float64)[:, None]
    v = np.arange(BLOCK, dtype=np.float64)[None, :]
    norm = np.sqrt(np.where(j == 0, 1.0, 2.0) / BLOCK)
    return (norm * np.cos(np.pi * (2 * v + 1) * j / (2 * BLOCK))).astype(np.float32)


def near_hop(hop, mirrored):
    chips = OWNERS // 2
    return [
        (2 * z + core, (z + (-hop if mirrored and core else hop)) % chips * 2 + core)
        for z in range(chips)
        for core in range(2)
    ]


def rep_groups(turn):
    groups = []
    for core in range(2):
        for z in range(OWNERS // 2):
            for i in range(SIDE):
                line = [(i * SIDE + k if core == turn else k * SIDE + i) for k in range(SIDE)]
                groups.append([rep * OWNERS + 2 * z + core for rep in line])
    return groups


def add_cores_kernel(plan_ref, parts_ref, *tile_refs):
    del plan_ref
    place = lax.axis_index("zl")
    for k, tile_ref in enumerate(tile_refs):
        rows = pl.ds(pl.multiple_of((place + k) % CHIPS * ROWS, ROWS), ROWS)
        tile_ref[...] = parts_ref[0, rows, :] + parts_ref[1, rows, :]


def plan_kernel(where_ref, counts_ref, plan_ref, branch_ref):
    plan_ref[0] = where_ref[0]
    plan_ref[1] = counts_ref[where_ref[1]]
    start = jnp.int32(0)
    reach = jnp.int32(0)
    first = jnp.int32(0)
    for i in range(OWNERS):
        if i % NEAR == 0:
            first = start - start % 128
        plan_ref[2 + i] = start
        start = start + counts_ref[i]
        reach = jnp.maximum(reach, start - first)
    branch_ref[0] = sum((reach > width).astype(jnp.int32) for width in WIDTHS[:-1])


def spread_kernel(width, plan_ref, own_ref, next_ref, across_ref, before_ref, out_ref, total_ref):
    total_ref[:, :BLOCKS] = (own_ref[...] + next_ref[...]) + (across_ref[...] + before_ref[...])
    total_ref[:, BLOCKS:] = jnp.zeros((ROWS, width), jnp.float32)
    for a in range(FAR):
        base = pl.multiple_of((plan_ref[2 + NEAR * a] // 128) * 128, 128)
        out_ref[a] = total_ref[:, pl.ds(base, width)]


def window_kernel(width, plan_ref, far_ref, parts_ref, out_ref, total_ref):
    total_ref[:, :width] = jnp.sum(parts_ref[...], axis=0)
    total_ref[:, width:] = jnp.zeros((ROWS, MOST + 128), jnp.float32)
    lane = lax.broadcasted_iota(jnp.int32, (ROWS, 128), 1)
    owner = far_ref[0] * NEAR
    first = (plan_ref[2 + owner] // 128) * 128
    for i in range(NEAR):
        start = plan_ref[2 + owner + i] - first
        base = pl.multiple_of((start // 128) * 128, 128)
        shift = start % 128
        tiles = [
            pltpu.roll(total_ref[:, pl.ds(base + 128 * t, 128)], (128 - shift) % 128, 1)
            for t in range(MOST // 128 + 1)
        ]
        for t in range(MOST // 128):
            out_ref[i, :, 128 * t : 128 * (t + 1)] = jnp.where(lane < 128 - shift, tiles[t], tiles[t + 1])


def deliver(width, plan, far, *near):
    smem = pl.BlockSpec(memory_space=pltpu.SMEM)
    whole = pl.BlockSpec(memory_space=pltpu.VMEM)
    small = pltpu.CompilerParams(vmem_limit_bytes=8 << 20)
    spread = pl.pallas_call(
        functools.partial(spread_kernel, width),
        out_shape=jax.ShapeDtypeStruct((FAR, ROWS, width), jnp.float32),
        in_specs=[smem] + [whole] * CHIPS,
        out_specs=whole,
        scratch_shapes=[pltpu.VMEM((ROWS, BLOCKS + width), jnp.float32)],
        compiler_params=small,
        name=f"spread_{width}",
    )(plan, *near)
    met = lax.all_to_all(spread, "zh", 0, 0, tiled=False)
    return pl.pallas_call(
        functools.partial(window_kernel, width),
        out_shape=jax.ShapeDtypeStruct((NEAR, ROWS, MOST), jnp.float32),
        in_specs=[smem, smem, whole],
        out_specs=whole,
        scratch_shapes=[pltpu.VMEM((ROWS, width + MOST + 128), jnp.float32)],
        compiler_params=small,
        name=f"windows_{width}",
    )(plan, far, met)


def owner_kernel(place_ref, parts_ref, momentum_ref, chosen_ref, table_ref, back_ref, momentum_out_ref, copies_ref):
    count = place_ref[1]
    live = lax.broadcasted_iota(jnp.int32, (BLOCK, MOST), 1) < count
    gradient = jnp.concatenate([parts_ref[b, c] for c in range(2) for b in range(CHIPS)], axis=0) * (1.0 / OWNERS)
    accumulated = jnp.where(live, momentum_decay * momentum_ref[0] + gradient, 0.0)
    coeffs = jnp.dot(table_ref[...], accumulated, precision=lax.Precision.HIGHEST, preferred_element_type=jnp.float32)
    chosen = chosen_ref[0]
    bit = jnp.left_shift(jnp.int32(1), chosen & 31)
    low = jnp.sum(jnp.where(chosen < 32, bit, 0), axis=0, keepdims=True)
    high = jnp.sum(jnp.where(chosen < 32, 0, bit), axis=0, keepdims=True)
    number = lax.broadcasted_iota(jnp.int32, (32, MOST), 0)
    listed = jnp.concatenate(
        [jnp.right_shift(jnp.broadcast_to(word, (32, MOST)), number) & 1 for word in (low, high)], axis=0
    )
    sparse = jnp.where(listed != 0, coeffs, 0.0)
    own = jnp.dot(back_ref[...], sparse, precision=lax.Precision.HIGHEST, preferred_element_type=jnp.float32)
    momentum_out_ref[0] = jnp.where(live, accumulated - own, 0.0)
    for r in range(SIDE):
        copies_ref[r] = own


def add_row_kernel(parts_ref, copies_ref):
    added = jnp.sum(parts_ref[...], axis=0)
    for r in range(SIDE):
        copies_ref[r] = added


def weights_kernel(place_ref, parts_ref, weights_ref, out_ref):
    live = lax.broadcasted_iota(jnp.int32, (BLOCK, MOST), 1) < place_ref[1]
    update = jnp.sum(parts_ref[...], axis=0) * (1.0 / GROUPS)
    out_ref[...] = jnp.where(live, weights_ref[...] - step_rate * update, 0.0)


def body(partials, owner_blocks, momentum, weights, selected):
    owner = lax.axis_index(FSDP)
    group = lax.axis_index(REP)
    far = lax.axis_index("zh").reshape(1)
    smem = pl.BlockSpec(memory_space=pltpu.SMEM)
    place, branch = pl.pallas_call(
        plan_kernel,
        out_shape=(jax.ShapeDtypeStruct((2 + OWNERS,), jnp.int32), jax.ShapeDtypeStruct((1,), jnp.int32)),
        in_specs=[smem, smem],
        out_specs=(smem, smem),
        compiler_params=pltpu.CompilerParams(vmem_limit_bytes=1 << 20),
        name="plan",
    )(jnp.stack([group, owner]).astype(jnp.int32), owner_blocks)
    whole = pl.BlockSpec(memory_space=pltpu.VMEM)

    halves = lax.all_to_all(partials.reshape(2, BLOCK // 2, BLOCKS), "core", 0, 0, tiled=False)
    tiles = pl.pallas_call(
        add_cores_kernel,
        out_shape=[jax.ShapeDtypeStruct((ROWS, BLOCKS), jnp.float32)] * CHIPS,
        in_specs=[pl.BlockSpec(memory_space=pl.ANY), whole],
        out_specs=[whole] * CHIPS,
        compiler_params=pltpu.CompilerParams(vmem_limit_bytes=8 << 20),
        name="add_cores",
    )(place, halves)
    across = lax.ppermute(tiles[2], FSDP, near_hop(-2, True))
    following = lax.ppermute(tiles[1], FSDP, near_hop(1, False))
    before = lax.ppermute(tiles[3], FSDP, near_hop(-1, False))
    near = (tiles[0], following, across, before)
    windows = lax.switch(branch[0], [functools.partial(deliver, width) for width in WIDTHS], place, far, *near)
    blocks = lax.all_to_all(windows, ("zl", "core"), 0, 0, tiled=False).reshape(CHIPS, 2, ROWS, MOST)

    table = dct_matrix()
    new_momentum, copies = pl.pallas_call(
        owner_kernel,
        out_shape=(
            jax.ShapeDtypeStruct((1, BLOCK, MOST), jnp.float32),
            jax.ShapeDtypeStruct((SIDE, BLOCK, MOST), jnp.float32),
        ),
        grid_spec=pltpu.PrefetchScalarGridSpec(
            num_scalar_prefetch=1,
            grid=(1,),
            in_specs=[
                pl.BlockSpec((CHIPS, 2, ROWS, MOST), lambda i, place: (0, 0, 0, 0)),
                pl.BlockSpec((1, BLOCK, MOST), lambda i, place: (0, 0, 0)),
                pl.BlockSpec((1, K, MOST), lambda i, place: (place[0], 0, 0)),
                pl.BlockSpec((BLOCK, BLOCK), lambda i, place: (0, 0)),
                pl.BlockSpec((BLOCK, BLOCK), lambda i, place: (0, 0)),
            ],
            out_specs=[
                pl.BlockSpec((1, BLOCK, MOST), lambda i, place: (0, 0, 0)),
                pl.BlockSpec((SIDE, BLOCK, MOST), lambda i, place: (0, 0, 0)),
            ],
        ),
        compiler_params=pltpu.CompilerParams(vmem_limit_bytes=16 << 20),
        name="owner_step",
    )(place, blocks, momentum, selected, jnp.asarray(table), jnp.asarray(table.T))
    row = lax.all_to_all(copies, REP + FSDP, 0, 0, axis_index_groups=rep_groups(0), tiled=False)
    copies = pl.pallas_call(
        add_row_kernel,
        out_shape=jax.ShapeDtypeStruct((SIDE, BLOCK, MOST), jnp.float32),
        in_specs=[whole],
        out_specs=whole,
        compiler_params=pltpu.CompilerParams(vmem_limit_bytes=8 << 20),
        name="add_row",
    )(row)
    everyone = lax.all_to_all(copies, REP + FSDP, 0, 0, axis_index_groups=rep_groups(1), tiled=False)
    new_weights = pl.pallas_call(
        weights_kernel,
        out_shape=jax.ShapeDtypeStruct((BLOCK, MOST), jnp.float32),
        in_specs=[pl.BlockSpec(memory_space=pltpu.SMEM), whole, whole],
        out_specs=whole,
        compiler_params=pltpu.CompilerParams(vmem_limit_bytes=8 << 20),
        name="weights_step",
    )(place, everyone, weights)
    return new_momentum, new_weights


def solution(mesh):
    fine = Mesh(mesh.devices.reshape(SIDE, SIDE, FAR, CHIPS, 2), REP + FSDP)
    return jax.shard_map(
        body,
        mesh=fine,
        in_specs=(P(REP, FSDP, None, None), P(), P(REP, None, FSDP), P(None, FSDP), P(None, None, FSDP)),
        out_specs=(P(REP, None, FSDP), P(None, FSDP)),
        check_vma=False,
    )
```

```python
import functools

import jax
import jax.numpy as jnp
import numpy as np
from jax import lax
from jax.experimental import pallas as pl
from jax.experimental.pallas import tpu as pltpu
from jax.sharding import Mesh, PartitionSpec as P

BLOCK = 64
K = 32
BLOCKS = 4096
MOST = 512
OWNERS = 32
GROUPS = 16
NEAR = 8
CHIPS = NEAR // 2
SIDE = 4
WIDTHS = (1280, 1408, 1536, 1664, 1792, 2048, 2560, 4096)
FAR = OWNERS // NEAR
ROWS = BLOCK // NEAR

REP = ("y", "x")
FSDP = ("zh", "zl", "core")

momentum_decay = 0.9
step_rate = 0.5


def dct_matrix():
    j = np.arange(BLOCK, dtype=np.float64)[:, None]
    v = np.arange(BLOCK, dtype=np.float64)[None, :]
    norm = np.sqrt(np.where(j == 0, 1.0, 2.0) / BLOCK)
    return (norm * np.cos(np.pi * (2 * v + 1) * j / (2 * BLOCK))).astype(np.float32)


def near_pairs(kind):
    chips = OWNERS // 2
    pairs = []
    for z in range(chips):
        for core in range(2):
            if kind == 2:
                hop = 2 if (z + 2 * core) % CHIPS < 2 else -2
            else:
                hop = 1 if (z + core + kind) % 2 == 0 else -1
            pairs.append((2 * z + core, (z + hop) % chips * 2 + core))
    return pairs


def rep_groups(turn):
    groups = []
    for core in range(2):
        for z in range(OWNERS // 2):
            for i in range(SIDE):
                line = [(i * SIDE + k if core == turn else k * SIDE + i) for k in range(SIDE)]
                groups.append([rep * OWNERS + 2 * z + core for rep in line])
    return groups


def add_cores_kernel(plan_ref, parts_ref, *tile_refs):
    del plan_ref
    place = lax.axis_index("zl")
    up = 1 + 2 * ((place + lax.axis_index("core")) % 2)
    for hop, tile_ref in zip((0, up, 4 - up, 2), tile_refs):
        rows = pl.ds(pl.multiple_of((place + hop) % CHIPS * ROWS, ROWS), ROWS)
        tile_ref[...] = parts_ref[0, rows, :] + parts_ref[1, rows, :]


def plan_kernel(where_ref, counts_ref, plan_ref, branch_ref):
    plan_ref[0] = where_ref[0]
    plan_ref[1] = counts_ref[where_ref[1]]
    start = jnp.int32(0)
    reach = jnp.int32(0)
    first = jnp.int32(0)
    for i in range(OWNERS):
        if i % NEAR == 0:
            first = start - start % 128
        plan_ref[2 + i] = start
        start = start + counts_ref[i]
        reach = jnp.maximum(reach, start - first)
    branch_ref[0] = sum((reach > width).astype(jnp.int32) for width in WIDTHS[:-1])


def spread_kernel(width, plan_ref, after_ref, own_ref, next_ref, other_ref, across_ref, out_ref, total_ref):
    del after_ref
    total_ref[:, :BLOCKS] = (own_ref[...] + next_ref[...]) + (other_ref[...] + across_ref[...])
    total_ref[:, BLOCKS:] = jnp.zeros((ROWS, width), jnp.float32)
    for a in range(FAR):
        base = pl.multiple_of((plan_ref[2 + NEAR * a] // 128) * 128, 128)
        out_ref[a] = total_ref[:, pl.ds(base, width)]


def window_kernel(width, plan_ref, far_ref, parts_ref, out_ref, total_ref):
    total_ref[:, :width] = jnp.sum(parts_ref[...], axis=0)
    total_ref[:, width:] = jnp.zeros((ROWS, MOST + 128), jnp.float32)
    lane = lax.broadcasted_iota(jnp.int32, (ROWS, 128), 1)
    owner = far_ref[0] * NEAR
    first = (plan_ref[2 + owner] // 128) * 128
    for i in range(NEAR):
        start = plan_ref[2 + owner + i] - first
        base = pl.multiple_of((start // 128) * 128, 128)
        shift = start % 128
        tiles = [
            pltpu.roll(total_ref[:, pl.ds(base + 128 * t, 128)], (128 - shift) % 128, 1)
            for t in range(MOST // 128 + 1)
        ]
        for t in range(MOST // 128):
            out_ref[i, :, 128 * t : 128 * (t + 1)] = jnp.where(lane < 128 - shift, tiles[t], tiles[t + 1])


def deliver(width, plan, far, after, *near):
    smem = pl.BlockSpec(memory_space=pltpu.SMEM)
    whole = pl.BlockSpec(memory_space=pltpu.VMEM)
    small = pltpu.CompilerParams(vmem_limit_bytes=8 << 20)
    spread = pl.pallas_call(
        functools.partial(spread_kernel, width),
        out_shape=jax.ShapeDtypeStruct((FAR, ROWS, width), jnp.float32),
        in_specs=[smem, pl.BlockSpec(memory_space=pl.ANY)] + [whole] * CHIPS,
        out_specs=whole,
        scratch_shapes=[pltpu.VMEM((ROWS, BLOCKS + width), jnp.float32)],
        compiler_params=small,
        name=f"spread_{width}",
    )(plan, after, *near)
    met = lax.all_to_all(spread, "zh", 0, 0, tiled=False)
    return pl.pallas_call(
        functools.partial(window_kernel, width),
        out_shape=jax.ShapeDtypeStruct((NEAR, ROWS, MOST), jnp.float32),
        in_specs=[smem, smem, whole],
        out_specs=whole,
        scratch_shapes=[pltpu.VMEM((ROWS, width + MOST + 128), jnp.float32)],
        compiler_params=small,
        name=f"windows_{width}",
    )(plan, far, met)


def prepare_kernel(place_ref, after_ref, momentum_ref, chosen_ref, table_ref, decayed_ref, listed_ref, sparse_ref, live_ref):
    del after_ref
    live = lax.broadcasted_iota(jnp.int32, (BLOCK, MOST), 1) < place_ref[1]
    decayed = jnp.where(live, momentum_decay * momentum_ref[0], 0.0)
    decayed_ref[...] = decayed
    live_ref[...] = live[:8].astype(jnp.float32)
    coeffs = jnp.dot(table_ref[...], decayed, precision=lax.Precision.HIGHEST, preferred_element_type=jnp.float32)
    chosen = chosen_ref[0]
    bit = jnp.left_shift(jnp.int32(1), chosen & 31)
    low = jnp.sum(jnp.where(chosen < 32, bit, 0), axis=0, keepdims=True)
    high = jnp.sum(jnp.where(chosen < 32, 0, bit), axis=0, keepdims=True)
    number = lax.broadcasted_iota(jnp.int32, (32, MOST), 0)
    listed = jnp.concatenate(
        [jnp.right_shift(jnp.broadcast_to(word, (32, MOST)), number) & 1 for word in (low, high)], axis=0
    )
    listed_ref[...] = listed
    sparse_ref[...] = jnp.where(listed != 0, coeffs, 0.0)


def owner_kernel(parts_ref, decayed_ref, listed_ref, sparse_ref, live_ref, table_ref, back_ref, left_ref, copies_ref):
    gathered = jnp.concatenate([parts_ref[b, c] for c in range(2) for b in range(CHIPS)], axis=0)
    gradient = jnp.where(live_ref[:1, :] != 0, gathered * (1.0 / OWNERS), 0.0)
    coeffs = jnp.dot(table_ref[...], gradient, precision=lax.Precision.HIGHEST, preferred_element_type=jnp.float32)
    sparse = sparse_ref[...] + jnp.where(listed_ref[...] != 0, coeffs, 0.0)
    own = jnp.dot(back_ref[...], sparse, precision=lax.Precision.HIGHEST, preferred_element_type=jnp.float32)
    left_ref[...] = decayed_ref[...] + gradient - own
    for r in range(SIDE):
        copies_ref[r] = own


def add_row_kernel(parts_ref, copies_ref):
    added = jnp.sum(parts_ref[...], axis=0)
    for r in range(SIDE):
        copies_ref[r] = added


def last_kernel(live_ref, left_ref, parts_ref, weights_ref, momentum_out_ref, out_ref):
    momentum_out_ref[0] = left_ref[...]
    update = jnp.sum(parts_ref[...], axis=0) * (1.0 / GROUPS)
    out_ref[...] = jnp.where(live_ref[:1, :] != 0, weights_ref[...] - step_rate * update, 0.0)


def body(partials, owner_blocks, momentum, weights, selected):
    owner = lax.axis_index(FSDP)
    group = lax.axis_index(REP)
    far = lax.axis_index("zh").reshape(1)
    smem = pl.BlockSpec(memory_space=pltpu.SMEM)
    place, branch = pl.pallas_call(
        plan_kernel,
        out_shape=(jax.ShapeDtypeStruct((2 + OWNERS,), jnp.int32), jax.ShapeDtypeStruct((1,), jnp.int32)),
        in_specs=[smem, smem],
        out_specs=(smem, smem),
        compiler_params=pltpu.CompilerParams(vmem_limit_bytes=1 << 20),
        name="plan",
    )(jnp.stack([group, owner]).astype(jnp.int32), owner_blocks)
    whole = pl.BlockSpec(memory_space=pltpu.VMEM)
    small = pltpu.CompilerParams(vmem_limit_bytes=8 << 20)

    halves = lax.all_to_all(partials.reshape(2, BLOCK // 2, BLOCKS), "core", 0, 0, tiled=False)
    tiles = pl.pallas_call(
        add_cores_kernel,
        out_shape=[jax.ShapeDtypeStruct((ROWS, BLOCKS), jnp.float32)] * CHIPS,
        in_specs=[pl.BlockSpec(memory_space=pl.ANY), whole],
        out_specs=[whole] * CHIPS,
        compiler_params=pltpu.CompilerParams(vmem_limit_bytes=8 << 20),
        name="add_cores",
    )(place, halves)
    table, back = jnp.asarray(dct_matrix()), jnp.asarray(dct_matrix().T)
    square = jax.ShapeDtypeStruct((BLOCK, MOST), jnp.float32)
    decayed, listed, sparse, live = pl.pallas_call(
        prepare_kernel,
        out_shape=(square, jax.ShapeDtypeStruct((BLOCK, MOST), jnp.int32), square, jax.ShapeDtypeStruct((8, MOST), jnp.float32)),
        grid_spec=pltpu.PrefetchScalarGridSpec(
            num_scalar_prefetch=1,
            grid=(1,),
            in_specs=[
                pl.BlockSpec(memory_space=pl.ANY),
                pl.BlockSpec((1, BLOCK, MOST), lambda i, place: (0, 0, 0)),
                pl.BlockSpec((1, K, MOST), lambda i, place: (place[0], 0, 0)),
                pl.BlockSpec((BLOCK, BLOCK), lambda i, place: (0, 0)),
            ],
            out_specs=[pl.BlockSpec((BLOCK, MOST), lambda i, place: (0, 0))] * 3 + [pl.BlockSpec((8, MOST), lambda i, place: (0, 0))],
        ),
        compiler_params=small,
        name="prepare",
    )(place, tiles[0], momentum, selected, table)
    near = [tiles[0]] + [lax.ppermute(tiles[1 + kind], FSDP, near_pairs(kind)) for kind in range(3)]
    windows = lax.switch(branch[0], [functools.partial(deliver, width) for width in WIDTHS], place, far, sparse, *near)
    blocks = lax.all_to_all(windows, ("zl", "core"), 0, 0, tiled=False).reshape(CHIPS, 2, ROWS, MOST)

    left, copies = pl.pallas_call(
        owner_kernel,
        out_shape=(square, jax.ShapeDtypeStruct((SIDE, BLOCK, MOST), jnp.float32)),
        in_specs=[whole] * 7,
        out_specs=(whole, whole),
        compiler_params=small,
        name="owner_step",
    )(blocks, decayed, listed, sparse, live, table, back)
    row = lax.all_to_all(copies, REP + FSDP, 0, 0, axis_index_groups=rep_groups(0), tiled=False)
    copies = pl.pallas_call(
        add_row_kernel,
        out_shape=jax.ShapeDtypeStruct((SIDE, BLOCK, MOST), jnp.float32),
        in_specs=[whole],
        out_specs=whole,
        compiler_params=pltpu.CompilerParams(vmem_limit_bytes=8 << 20),
        name="add_row",
    )(row)
    everyone = lax.all_to_all(copies, REP + FSDP, 0, 0, axis_index_groups=rep_groups(1), tiled=False)
    new_momentum, new_weights = pl.pallas_call(
        last_kernel,
        out_shape=(jax.ShapeDtypeStruct((1, BLOCK, MOST), jnp.float32), square),
        in_specs=[whole] * 4,
        out_specs=(whole, whole),
        compiler_params=small,
        name="weights_step",
    )(live, left, everyone, weights)
    return new_momentum, new_weights


def solution(mesh):
    fine = Mesh(mesh.devices.reshape(SIDE, SIDE, FAR, CHIPS, 2), REP + FSDP)
    return jax.shard_map(
        body,
        mesh=fine,
        in_specs=(P(REP, FSDP, None, None), P(), P(REP, None, FSDP), P(None, FSDP), P(None, None, FSDP)),
        out_specs=(P(REP, None, FSDP), P(None, FSDP)),
        check_vma=False,
    )
```

```python
import functools

import jax
import jax.numpy as jnp
import numpy as np
from jax import lax
from jax.experimental import pallas as pl
from jax.experimental.pallas import tpu as pltpu
from jax.sharding import Mesh, PartitionSpec as P

BLOCK = 64
K = 32
BLOCKS = 4096
MOST = 512
OWNERS = 32
GROUPS = 16
NEAR = 8
CHIPS = NEAR // 2
SIDE = 4
WIDTHS = (1280, 1408, 1536, 1664, 1792, 2048, 2560, 4096)
FAR = OWNERS // NEAR
ROWS = BLOCK // NEAR

REP = ("y", "x")
FSDP = ("zh", "zl", "core")

momentum_decay = 0.9
step_rate = 0.5


def dct_matrix():
    j = np.arange(BLOCK, dtype=np.float64)[:, None]
    v = np.arange(BLOCK, dtype=np.float64)[None, :]
    norm = np.sqrt(np.where(j == 0, 1.0, 2.0) / BLOCK)
    return (norm * np.cos(np.pi * (2 * v + 1) * j / (2 * BLOCK))).astype(np.float32)


def near_pairs(kind):
    chips = OWNERS // 2
    pairs = []
    for z in range(chips):
        for core in range(2):
            if kind == 2:
                hop = 2 if (z + 2 * core) % CHIPS < 2 else -2
            else:
                hop = 1 if (z + core + kind) % 2 == 0 else -1
            pairs.append((2 * z + core, (z + hop) % chips * 2 + core))
    return pairs


def rep_groups(turn):
    groups = []
    for core in range(2):
        for z in range(OWNERS // 2):
            for i in range(SIDE):
                line = [(i * SIDE + k if core == turn else k * SIDE + i) for k in range(SIDE)]
                groups.append([rep * OWNERS + 2 * z + core for rep in line])
    return groups


def add_cores_kernel(plan_ref, parts_ref, *tile_refs):
    del plan_ref
    place = lax.axis_index("zl")
    up = 1 + 2 * ((place + lax.axis_index("core")) % 2)
    for hop, tile_ref in zip((0, up, 4 - up, 2), tile_refs):
        rows = pl.ds(pl.multiple_of((place + hop) % CHIPS * ROWS, ROWS), ROWS)
        tile_ref[...] = parts_ref[0, rows, :] + parts_ref[1, rows, :]


def plan_kernel(where_ref, counts_ref, plan_ref, branch_ref, offsets_ref):
    plan_ref[0] = where_ref[0]
    plan_ref[1] = counts_ref[where_ref[1]]
    far = where_ref[1] // NEAR
    lane = lax.broadcasted_iota(jnp.int32, (8, 128), 1)
    offsets = jnp.zeros((8, 128), jnp.int32)
    start = jnp.int32(0)
    reach = jnp.int32(0)
    first = jnp.int32(0)
    for i in range(OWNERS):
        if i % NEAR == 0:
            first = start - start % 128
            offsets = jnp.where(lane == i // NEAR, first, offsets)
        here = (lane == FAR + i % NEAR) & (far == i // NEAR)
        offsets = jnp.where(here, start - first, offsets)
        start = start + counts_ref[i]
        reach = jnp.maximum(reach, start - first)
    branch_ref[0] = sum((reach > width).astype(jnp.int32) for width in WIDTHS[:-1])
    offsets_ref[...] = offsets


def spread_kernel(width, offsets_ref, after_ref, own_ref, next_ref, other_ref, across_ref, out_ref, total_ref):
    del after_ref
    total_ref[:, :BLOCKS] = (own_ref[...] + next_ref[...]) + (other_ref[...] + across_ref[...])
    total_ref[:, BLOCKS:] = jnp.zeros((ROWS, width), jnp.float32)
    for a in range(FAR):
        base = pl.multiple_of(offsets_ref[0, a], 128)
        out_ref[a] = total_ref[:, pl.ds(base, width)]


def window_kernel(width, offsets_ref, parts_ref, out_ref, total_ref):
    total_ref[:, :width] = jnp.sum(parts_ref[...], axis=0)
    total_ref[:, width:] = jnp.zeros((ROWS, MOST + 128), jnp.float32)
    lane = lax.broadcasted_iota(jnp.int32, (ROWS, 128), 1)
    for i in range(NEAR):
        start = offsets_ref[0, FAR + i]
        base = pl.multiple_of((start // 128) * 128, 128)
        shift = start % 128
        tiles = [
            pltpu.roll(total_ref[:, pl.ds(base + 128 * t, 128)], (128 - shift) % 128, 1)
            for t in range(MOST // 128 + 1)
        ]
        for t in range(MOST // 128):
            out_ref[i, :, 128 * t : 128 * (t + 1)] = jnp.where(lane < 128 - shift, tiles[t], tiles[t + 1])


def deliver(width, offsets, after, *near):
    whole = pl.BlockSpec(memory_space=pltpu.VMEM)
    small = pltpu.CompilerParams(vmem_limit_bytes=8 << 20)
    spread = pl.pallas_call(
        functools.partial(spread_kernel, width),
        out_shape=jax.ShapeDtypeStruct((FAR, ROWS, width), jnp.float32),
        in_specs=[whole, pl.BlockSpec(memory_space=pl.ANY)] + [whole] * CHIPS,
        out_specs=whole,
        scratch_shapes=[pltpu.VMEM((ROWS, BLOCKS + width), jnp.float32)],
        compiler_params=small,
        name=f"spread_{width}",
    )(offsets, after, *near)
    met = lax.all_to_all(spread, "zh", 0, 0, tiled=False)
    return pl.pallas_call(
        functools.partial(window_kernel, width),
        out_shape=jax.ShapeDtypeStruct((NEAR, ROWS, MOST), jnp.float32),
        in_specs=[whole, whole],
        out_specs=whole,
        scratch_shapes=[pltpu.VMEM((ROWS, width + MOST + 128), jnp.float32)],
        compiler_params=small,
        name=f"windows_{width}",
    )(offsets, met)


def prepare_kernel(place_ref, after_ref, momentum_ref, chosen_ref, table_ref, decayed_ref, listed_ref, sparse_ref, live_ref):
    del after_ref
    live = lax.broadcasted_iota(jnp.int32, (BLOCK, MOST), 1) < place_ref[1]
    decayed = jnp.where(live, momentum_decay * momentum_ref[0], 0.0)
    decayed_ref[...] = decayed
    live_ref[...] = live[:8].astype(jnp.float32)
    coeffs = jnp.dot(table_ref[...], decayed, precision=lax.Precision.HIGHEST, preferred_element_type=jnp.float32)
    chosen = chosen_ref[0]
    bit = jnp.left_shift(jnp.int32(1), chosen & 31)
    low = jnp.sum(jnp.where(chosen < 32, bit, 0), axis=0, keepdims=True)
    high = jnp.sum(jnp.where(chosen < 32, 0, bit), axis=0, keepdims=True)
    number = lax.broadcasted_iota(jnp.int32, (32, MOST), 0)
    listed = jnp.concatenate(
        [jnp.right_shift(jnp.broadcast_to(word, (32, MOST)), number) & 1 for word in (low, high)], axis=0
    )
    listed_ref[...] = listed
    sparse_ref[...] = jnp.where(listed != 0, coeffs, 0.0)


def owner_kernel(parts_ref, decayed_ref, listed_ref, sparse_ref, live_ref, table_ref, back_ref, left_ref, copies_ref):
    gathered = jnp.concatenate([parts_ref[b, c] for c in range(2) for b in range(CHIPS)], axis=0)
    gradient = jnp.where(live_ref[:1, :] != 0, gathered * (1.0 / OWNERS), 0.0)
    coeffs = jnp.dot(table_ref[...], gradient, precision=lax.Precision.HIGHEST, preferred_element_type=jnp.float32)
    sparse = sparse_ref[...] + jnp.where(listed_ref[...] != 0, coeffs, 0.0)
    own = jnp.dot(back_ref[...], sparse, precision=lax.Precision.HIGHEST, preferred_element_type=jnp.float32)
    left_ref[...] = decayed_ref[...] + gradient - own
    for r in range(SIDE):
        copies_ref[r] = own


def add_row_kernel(parts_ref, copies_ref):
    added = jnp.sum(parts_ref[...], axis=0)
    for r in range(SIDE):
        copies_ref[r] = added


def last_kernel(live_ref, left_ref, parts_ref, weights_ref, momentum_out_ref, out_ref):
    momentum_out_ref[0] = left_ref[...]
    update = jnp.sum(parts_ref[...], axis=0) * (1.0 / GROUPS)
    out_ref[...] = jnp.where(live_ref[:1, :] != 0, weights_ref[...] - step_rate * update, 0.0)


def body(partials, owner_blocks, momentum, weights, selected):
    owner = lax.axis_index(FSDP)
    group = lax.axis_index(REP)
    smem = pl.BlockSpec(memory_space=pltpu.SMEM)
    whole = pl.BlockSpec(memory_space=pltpu.VMEM)
    small = pltpu.CompilerParams(vmem_limit_bytes=8 << 20)
    place, branch, offsets = pl.pallas_call(
        plan_kernel,
        out_shape=tuple(jax.ShapeDtypeStruct(shape, jnp.int32) for shape in ((2,), (1,), (8, 128))),
        in_specs=[smem, smem],
        out_specs=(smem, smem, whole),
        compiler_params=pltpu.CompilerParams(vmem_limit_bytes=1 << 20),
        name="plan",
    )(jnp.stack([group, owner]).astype(jnp.int32), owner_blocks)
    halves = lax.all_to_all(partials.reshape(2, BLOCK // 2, BLOCKS), "core", 0, 0, tiled=False)
    tiles = pl.pallas_call(
        add_cores_kernel,
        out_shape=[jax.ShapeDtypeStruct((ROWS, BLOCKS), jnp.float32)] * CHIPS,
        in_specs=[pl.BlockSpec(memory_space=pl.ANY), whole],
        out_specs=[whole] * CHIPS,
        compiler_params=pltpu.CompilerParams(vmem_limit_bytes=8 << 20),
        name="add_cores",
    )(place, halves)
    table, back = jnp.asarray(dct_matrix()), jnp.asarray(dct_matrix().T)
    square = jax.ShapeDtypeStruct((BLOCK, MOST), jnp.float32)
    decayed, listed, sparse, live = pl.pallas_call(
        prepare_kernel,
        out_shape=(square, jax.ShapeDtypeStruct((BLOCK, MOST), jnp.int32), square, jax.ShapeDtypeStruct((8, MOST), jnp.float32)),
        grid_spec=pltpu.PrefetchScalarGridSpec(
            num_scalar_prefetch=1,
            grid=(1,),
            in_specs=[
                pl.BlockSpec(memory_space=pl.ANY),
                pl.BlockSpec((1, BLOCK, MOST), lambda i, place: (0, 0, 0)),
                pl.BlockSpec((1, K, MOST), lambda i, place: (place[0], 0, 0)),
                pl.BlockSpec((BLOCK, BLOCK), lambda i, place: (0, 0)),
            ],
            out_specs=[pl.BlockSpec((BLOCK, MOST), lambda i, place: (0, 0))] * 3 + [pl.BlockSpec((8, MOST), lambda i, place: (0, 0))],
        ),
        compiler_params=small,
        name="prepare",
    )(place, tiles[0], momentum, selected, table)
    near = [tiles[0]] + [lax.ppermute(tiles[1 + kind], FSDP, near_pairs(kind)) for kind in range(3)]
    windows = lax.switch(branch[0], [functools.partial(deliver, width) for width in WIDTHS], offsets, sparse, *near)
    blocks = lax.all_to_all(windows, ("zl", "core"), 0, 0, tiled=False).reshape(CHIPS, 2, ROWS, MOST)

    left, copies = pl.pallas_call(
        owner_kernel,
        out_shape=(square, jax.ShapeDtypeStruct((SIDE, BLOCK, MOST), jnp.float32)),
        in_specs=[whole] * 7,
        out_specs=(whole, whole),
        compiler_params=small,
        name="owner_step",
    )(blocks, decayed, listed, sparse, live, table, back)
    row = lax.all_to_all(copies, REP + FSDP, 0, 0, axis_index_groups=rep_groups(0), tiled=False)
    copies = pl.pallas_call(
        add_row_kernel,
        out_shape=jax.ShapeDtypeStruct((SIDE, BLOCK, MOST), jnp.float32),
        in_specs=[whole],
        out_specs=whole,
        compiler_params=pltpu.CompilerParams(vmem_limit_bytes=8 << 20),
        name="add_row",
    )(row)
    everyone = lax.all_to_all(copies, REP + FSDP, 0, 0, axis_index_groups=rep_groups(1), tiled=False)
    new_momentum, new_weights = pl.pallas_call(
        last_kernel,
        out_shape=(jax.ShapeDtypeStruct((1, BLOCK, MOST), jnp.float32), square),
        in_specs=[whole] * 4,
        out_specs=(whole, whole),
        compiler_params=small,
        name="weights_step",
    )(live, left, everyone, weights)
    return new_momentum, new_weights


def solution(mesh):
    fine = Mesh(mesh.devices.reshape(SIDE, SIDE, FAR, CHIPS, 2), REP + FSDP)
    return jax.shard_map(
        body,
        mesh=fine,
        in_specs=(P(REP, FSDP, None, None), P(), P(REP, None, FSDP), P(None, FSDP), P(None, None, FSDP)),
        out_specs=(P(REP, None, FSDP), P(None, FSDP)),
        check_vma=False,
    )
```

```python
import functools

import jax
import jax.numpy as jnp
import numpy as np
from jax import lax
from jax.experimental import pallas as pl
from jax.experimental.pallas import tpu as pltpu
from jax.sharding import Mesh, PartitionSpec as P

BLOCK = 64
K = 32
BLOCKS = 4096
MOST = 512
OWNERS = 32
GROUPS = 16
NEAR = 8
CHIPS = NEAR // 2
SIDE = 4
WIDTHS = (1280, 1408, 1536, 1664, 1792, 1920, 2048, 2304, 2560, 4096)
FAR = OWNERS // NEAR
ROWS = BLOCK // NEAR

REP = ("y", "x")
FSDP = ("zh", "zl", "core")

momentum_decay = 0.9
step_rate = 0.5


def dct_matrix():
    j = np.arange(BLOCK, dtype=np.float64)[:, None]
    v = np.arange(BLOCK, dtype=np.float64)[None, :]
    norm = np.sqrt(np.where(j == 0, 1.0, 2.0) / BLOCK)
    return (norm * np.cos(np.pi * (2 * v + 1) * j / (2 * BLOCK))).astype(np.float32)


def near_pairs(kind):
    chips = OWNERS // 2
    pairs = []
    for z in range(chips):
        for core in range(2):
            if kind == 2:
                hop = 2 if (z + 2 * core) % CHIPS < 2 else -2
            else:
                hop = 1 if (z + core + kind) % 2 == 0 else -1
            pairs.append((2 * z + core, (z + hop) % chips * 2 + core))
    return pairs


def rep_groups(turn):
    groups = []
    for core in range(2):
        for z in range(OWNERS // 2):
            for i in range(SIDE):
                line = [(i * SIDE + k if core == turn else k * SIDE + i) for k in range(SIDE)]
                groups.append([rep * OWNERS + 2 * z + core for rep in line])
    return groups


def other_half_kernel(partials_ref, out_ref, done):
    rows = pl.ds(pl.multiple_of((1 - lax.axis_index("core")) * (BLOCK // 2), BLOCK // 2), BLOCK // 2)
    copy = pltpu.make_async_copy(partials_ref.at[rows, :], out_ref, done)
    copy.start()
    copy.wait()


def add_cores_kernel(plan_ref, partials_ref, received_ref, *tile_refs):
    del plan_ref
    place = lax.axis_index("zl")
    core = lax.axis_index("core")
    up = 1 + 2 * ((place + core) % 2)
    for hop, tile_ref in zip((0, up, 4 - up, 2), tile_refs):
        row = (place + hop) % CHIPS * ROWS
        here = pl.ds(pl.multiple_of(core * (BLOCK // 2) + row, ROWS), ROWS)
        tile_ref[...] = partials_ref[here, :] + received_ref[pl.ds(pl.multiple_of(row, ROWS), ROWS), :]


def plan_kernel(where_ref, counts_ref, plan_ref, branch_ref, offsets_ref):
    plan_ref[0] = where_ref[0]
    plan_ref[1] = counts_ref[where_ref[1]]
    far = where_ref[1] // NEAR
    lane = lax.broadcasted_iota(jnp.int32, (8, 128), 1)
    offsets = jnp.zeros((8, 128), jnp.int32)
    start = jnp.int32(0)
    reach = jnp.int32(0)
    first = jnp.int32(0)
    for i in range(OWNERS):
        if i % NEAR == 0:
            first = start - start % 128
            offsets = jnp.where(lane == i // NEAR, first, offsets)
        here = (lane == FAR + i % NEAR) & (far == i // NEAR)
        offsets = jnp.where(here, start - first, offsets)
        start = start + counts_ref[i]
        reach = jnp.maximum(reach, start - first)
    branch_ref[0] = sum((reach > width).astype(jnp.int32) for width in WIDTHS[:-1])
    offsets_ref[...] = offsets


def spread_kernel(width, offsets_ref, after_ref, own_ref, next_ref, other_ref, across_ref, out_ref, total_ref):
    del after_ref
    total_ref[:, :BLOCKS] = (own_ref[...] + next_ref[...]) + (other_ref[...] + across_ref[...])
    total_ref[:, BLOCKS:] = jnp.zeros((ROWS, width), jnp.float32)
    for a in range(FAR):
        base = pl.multiple_of(offsets_ref[0, a], 128)
        out_ref[a] = total_ref[:, pl.ds(base, width)]


def window_kernel(width, offsets_ref, parts_ref, out_ref, total_ref):
    total_ref[:, :width] = jnp.sum(parts_ref[...], axis=0)
    total_ref[:, width:] = jnp.zeros((ROWS, MOST + 128), jnp.float32)
    lane = lax.broadcasted_iota(jnp.int32, (ROWS, 128), 1)
    for i in range(NEAR):
        start = offsets_ref[0, FAR + i]
        base = pl.multiple_of((start // 128) * 128, 128)
        shift = start % 128
        tiles = [
            pltpu.roll(total_ref[:, pl.ds(base + 128 * t, 128)], (128 - shift) % 128, 1)
            for t in range(MOST // 128 + 1)
        ]
        for t in range(MOST // 128):
            out_ref[i, :, 128 * t : 128 * (t + 1)] = jnp.where(lane < 128 - shift, tiles[t], tiles[t + 1])


def deliver(width, offsets, after, *near):
    whole = pl.BlockSpec(memory_space=pltpu.VMEM)
    small = pltpu.CompilerParams(vmem_limit_bytes=8 << 20)
    spread = pl.pallas_call(
        functools.partial(spread_kernel, width),
        out_shape=jax.ShapeDtypeStruct((FAR, ROWS, width), jnp.float32),
        in_specs=[whole, pl.BlockSpec(memory_space=pl.ANY)] + [whole] * CHIPS,
        out_specs=whole,
        scratch_shapes=[pltpu.VMEM((ROWS, BLOCKS + width), jnp.float32)],
        compiler_params=small,
        name=f"spread_{width}",
    )(offsets, after, *near)
    met = lax.all_to_all(spread, "zh", 0, 0, tiled=False)
    return pl.pallas_call(
        functools.partial(window_kernel, width),
        out_shape=jax.ShapeDtypeStruct((NEAR, ROWS, MOST), jnp.float32),
        in_specs=[whole, whole],
        out_specs=whole,
        scratch_shapes=[pltpu.VMEM((ROWS, width + MOST + 128), jnp.float32)],
        compiler_params=small,
        name=f"windows_{width}",
    )(offsets, met)


def prepare_kernel(place_ref, after_ref, momentum_ref, chosen_ref, table_ref, decayed_ref, listed_ref, sparse_ref, live_ref):
    del after_ref
    live = lax.broadcasted_iota(jnp.int32, (BLOCK, MOST), 1) < place_ref[1]
    decayed = jnp.where(live, momentum_decay * momentum_ref[0], 0.0)
    decayed_ref[...] = decayed
    live_ref[...] = live[:8].astype(jnp.float32)
    coeffs = jnp.dot(table_ref[...], decayed, precision=lax.Precision.HIGHEST, preferred_element_type=jnp.float32)
    chosen = chosen_ref[0]
    bit = jnp.left_shift(jnp.int32(1), chosen & 31)
    low = jnp.sum(jnp.where(chosen < 32, bit, 0), axis=0, keepdims=True)
    high = jnp.sum(jnp.where(chosen < 32, 0, bit), axis=0, keepdims=True)
    number = lax.broadcasted_iota(jnp.int32, (32, MOST), 0)
    listed = jnp.concatenate(
        [jnp.right_shift(jnp.broadcast_to(word, (32, MOST)), number) & 1 for word in (low, high)], axis=0
    )
    listed_ref[...] = listed
    sparse_ref[...] = jnp.where(listed != 0, coeffs, 0.0)


def owner_kernel(parts_ref, decayed_ref, listed_ref, sparse_ref, live_ref, table_ref, back_ref, left_ref, copies_ref):
    gathered = jnp.concatenate([parts_ref[b, c] for c in range(2) for b in range(CHIPS)], axis=0)
    gradient = jnp.where(live_ref[:1, :] != 0, gathered * (1.0 / OWNERS), 0.0)
    coeffs = jnp.dot(table_ref[...], gradient, precision=lax.Precision.HIGHEST, preferred_element_type=jnp.float32)
    sparse = sparse_ref[...] + jnp.where(listed_ref[...] != 0, coeffs, 0.0)
    own = jnp.dot(back_ref[...], sparse, precision=lax.Precision.HIGHEST, preferred_element_type=jnp.float32)
    left_ref[...] = decayed_ref[...] + gradient - own
    for r in range(SIDE):
        copies_ref[r] = own


def add_row_kernel(parts_ref, copies_ref):
    added = jnp.sum(parts_ref[...], axis=0)
    for r in range(SIDE):
        copies_ref[r] = added


def last_kernel(live_ref, left_ref, parts_ref, weights_ref, momentum_out_ref, out_ref):
    momentum_out_ref[0] = left_ref[...]
    update = jnp.sum(parts_ref[...], axis=0) * (1.0 / GROUPS)
    out_ref[...] = jnp.where(live_ref[:1, :] != 0, weights_ref[...] - step_rate * update, 0.0)


def body(partials, owner_blocks, momentum, weights, selected):
    owner = lax.axis_index(FSDP)
    group = lax.axis_index(REP)
    smem = pl.BlockSpec(memory_space=pltpu.SMEM)
    whole = pl.BlockSpec(memory_space=pltpu.VMEM)
    small = pltpu.CompilerParams(vmem_limit_bytes=8 << 20)
    place, branch, offsets = pl.pallas_call(
        plan_kernel,
        out_shape=tuple(jax.ShapeDtypeStruct(shape, jnp.int32) for shape in ((2,), (1,), (8, 128))),
        in_specs=[smem, smem],
        out_specs=(smem, smem, whole),
        compiler_params=pltpu.CompilerParams(vmem_limit_bytes=1 << 20),
        name="plan",
    )(jnp.stack([group, owner]).astype(jnp.int32), owner_blocks)
    partials = partials.reshape(BLOCK, BLOCKS)
    leaving = pl.pallas_call(
        other_half_kernel,
        out_shape=jax.ShapeDtypeStruct((BLOCK // 2, BLOCKS), jnp.float32),
        in_specs=[pl.BlockSpec(memory_space=pl.ANY)],
        out_specs=whole,
        scratch_shapes=[pltpu.SemaphoreType.DMA],
        compiler_params=small,
        name="other_half",
    )(partials)
    received = lax.ppermute(leaving, "core", [(0, 1), (1, 0)])
    tiles = pl.pallas_call(
        add_cores_kernel,
        out_shape=[jax.ShapeDtypeStruct((ROWS, BLOCKS), jnp.float32)] * CHIPS,
        in_specs=[pl.BlockSpec(memory_space=pl.ANY), whole, whole],
        out_specs=[whole] * CHIPS,
        compiler_params=pltpu.CompilerParams(vmem_limit_bytes=8 << 20),
        name="add_cores",
    )(place, partials, received)
    table, back = jnp.asarray(dct_matrix()), jnp.asarray(dct_matrix().T)
    square = jax.ShapeDtypeStruct((BLOCK, MOST), jnp.float32)
    decayed, listed, sparse, live = pl.pallas_call(
        prepare_kernel,
        out_shape=(square, jax.ShapeDtypeStruct((BLOCK, MOST), jnp.int32), square, jax.ShapeDtypeStruct((8, MOST), jnp.float32)),
        grid_spec=pltpu.PrefetchScalarGridSpec(
            num_scalar_prefetch=1,
            grid=(1,),
            in_specs=[
                pl.BlockSpec(memory_space=pl.ANY),
                pl.BlockSpec((1, BLOCK, MOST), lambda i, place: (0, 0, 0)),
                pl.BlockSpec((1, K, MOST), lambda i, place: (place[0], 0, 0)),
                pl.BlockSpec((BLOCK, BLOCK), lambda i, place: (0, 0)),
            ],
            out_specs=[pl.BlockSpec((BLOCK, MOST), lambda i, place: (0, 0))] * 3 + [pl.BlockSpec((8, MOST), lambda i, place: (0, 0))],
        ),
        compiler_params=small,
        name="prepare",
    )(place, tiles[0], momentum, selected, table)
    near = [tiles[0]] + [lax.ppermute(tiles[1 + kind], FSDP, near_pairs(kind)) for kind in range(3)]
    windows = lax.switch(branch[0], [functools.partial(deliver, width) for width in WIDTHS], offsets, sparse, *near)
    blocks = lax.all_to_all(windows, ("zl", "core"), 0, 0, tiled=False).reshape(CHIPS, 2, ROWS, MOST)

    left, copies = pl.pallas_call(
        owner_kernel,
        out_shape=(square, jax.ShapeDtypeStruct((SIDE, BLOCK, MOST), jnp.float32)),
        in_specs=[whole] * 7,
        out_specs=(whole, whole),
        compiler_params=small,
        name="owner_step",
    )(blocks, decayed, listed, sparse, live, table, back)
    row = lax.all_to_all(copies, REP + FSDP, 0, 0, axis_index_groups=rep_groups(0), tiled=False)
    copies = pl.pallas_call(
        add_row_kernel,
        out_shape=jax.ShapeDtypeStruct((SIDE, BLOCK, MOST), jnp.float32),
        in_specs=[whole],
        out_specs=whole,
        compiler_params=pltpu.CompilerParams(vmem_limit_bytes=8 << 20),
        name="add_row",
    )(row)
    everyone = lax.all_to_all(copies, REP + FSDP, 0, 0, axis_index_groups=rep_groups(1), tiled=False)
    new_momentum, new_weights = pl.pallas_call(
        last_kernel,
        out_shape=(jax.ShapeDtypeStruct((1, BLOCK, MOST), jnp.float32), square),
        in_specs=[whole] * 4,
        out_specs=(whole, whole),
        compiler_params=small,
        name="weights_step",
    )(live, left, everyone, weights)
    return new_momentum, new_weights


def solution(mesh):
    fine = Mesh(mesh.devices.reshape(SIDE, SIDE, FAR, CHIPS, 2), REP + FSDP)
    return jax.shard_map(
        body,
        mesh=fine,
        in_specs=(P(REP, FSDP, None, None), P(), P(REP, None, FSDP), P(None, FSDP), P(None, None, FSDP)),
        out_specs=(P(REP, None, FSDP), P(None, FSDP)),
        check_vma=False,
    )
```

```python
import functools

import jax
import jax.numpy as jnp
import numpy as np
from jax import lax
from jax.experimental import pallas as pl
from jax.experimental.pallas import tpu as pltpu
from jax.sharding import Mesh, PartitionSpec as P

BLOCK = 64
K = 32
BLOCKS = 4096
MOST = 512
OWNERS = 32
GROUPS = 16
NEAR = 8
CHIPS = NEAR // 2
SIDE = 4
WIDTHS = (1280, 1408, 1536, 1664, 1792, 1920, 2048, 2304, 2560, 4096)
FAR = OWNERS // NEAR
ROWS = BLOCK // NEAR

REP = ("y", "x")
FSDP = ("zh", "zl", "core")

momentum_decay = 0.9
step_rate = 0.5


def dct_matrix():
    j = np.arange(BLOCK, dtype=np.float64)[:, None]
    v = np.arange(BLOCK, dtype=np.float64)[None, :]
    norm = np.sqrt(np.where(j == 0, 1.0, 2.0) / BLOCK)
    return (norm * np.cos(np.pi * (2 * v + 1) * j / (2 * BLOCK))).astype(np.float32)


def near_pairs(kind):
    chips = OWNERS // 2
    pairs = []
    for z in range(chips):
        for core in range(2):
            if kind == 2:
                hop = 2 if (z + 2 * core) % CHIPS < 2 else -2
            else:
                hop = 1 if (z + core + kind) % 2 == 0 else -1
            pairs.append((2 * z + core, (z + hop) % chips * 2 + core))
    return pairs


def far_hop(group, core, kind):
    if kind == 0:
        return (group + 2) % FAR
    turned = (core + kind + 1) % 2
    return (((group + FAR - turned) % FAR ^ 1) + turned) % FAR


def far_pairs(kind):
    pairs = []
    for group in range(FAR):
        for f in range(NEAR):
            pairs.append((group * NEAR + f, far_hop(group, f % 2, kind) * NEAR + f))
    return pairs


def rep_groups(turn):
    groups = []
    for core in range(2):
        for z in range(OWNERS // 2):
            for i in range(SIDE):
                line = [(i * SIDE + k if core == turn else k * SIDE + i) for k in range(SIDE)]
                groups.append([rep * OWNERS + 2 * z + core for rep in line])
    return groups


def other_half_kernel(partials_ref, out_ref, done):
    rows = pl.ds(pl.multiple_of((1 - lax.axis_index("core")) * (BLOCK // 2), BLOCK // 2), BLOCK // 2)
    copy = pltpu.make_async_copy(partials_ref.at[rows, :], out_ref, done)
    copy.start()
    copy.wait()


def add_cores_kernel(plan_ref, partials_ref, received_ref, *tile_refs):
    del plan_ref
    place = lax.axis_index("zl")
    core = lax.axis_index("core")
    up = 1 + 2 * ((place + core) % 2)
    for hop, tile_ref in zip((0, up, 4 - up, 2), tile_refs):
        row = (place + hop) % CHIPS * ROWS
        here = pl.ds(pl.multiple_of(core * (BLOCK // 2) + row, ROWS), ROWS)
        tile_ref[...] = partials_ref[here, :] + received_ref[pl.ds(pl.multiple_of(row, ROWS), ROWS), :]


def plan_kernel(where_ref, counts_ref, plan_ref, branch_ref, offsets_ref):
    plan_ref[0] = where_ref[0]
    plan_ref[1] = counts_ref[where_ref[1]]
    far = where_ref[1] // NEAR
    hops = [far] + [far_hop(far, where_ref[1] % 2, kind) for kind in range(FAR - 1)]
    lane = lax.broadcasted_iota(jnp.int32, (8, 128), 1)
    offsets = jnp.zeros((8, 128), jnp.int32)
    start = jnp.int32(0)
    reach = jnp.int32(0)
    first = jnp.int32(0)
    for i in range(OWNERS):
        if i % NEAR == 0:
            first = start - start % 128
            for k, hop in enumerate(hops):
                offsets = jnp.where((lane == k) & (hop == i // NEAR), first, offsets)
        here = (lane == FAR + i % NEAR) & (far == i // NEAR)
        offsets = jnp.where(here, start - first, offsets)
        start = start + counts_ref[i]
        reach = jnp.maximum(reach, start - first)
    branch_ref[0] = sum((reach > width).astype(jnp.int32) for width in WIDTHS[:-1])
    offsets_ref[...] = offsets


def spread_kernel(width, offsets_ref, after_ref, own_ref, next_ref, other_ref, across_ref, *refs):
    del after_ref
    *out_refs, total_ref = refs
    total_ref[:, :BLOCKS] = (own_ref[...] + next_ref[...]) + (other_ref[...] + across_ref[...])
    total_ref[:, BLOCKS:] = jnp.zeros((ROWS, width), jnp.float32)
    for k, out_ref in enumerate(out_refs):
        base = pl.multiple_of(offsets_ref[0, k], 128)
        out_ref[...] = total_ref[:, pl.ds(base, width)]


def window_kernel(width, offsets_ref, own_ref, across_ref, next_ref, other_ref, out_ref, total_ref):
    total_ref[:, :width] = (own_ref[...] + across_ref[...]) + (next_ref[...] + other_ref[...])
    total_ref[:, width:] = jnp.zeros((ROWS, MOST + 128), jnp.float32)
    lane = lax.broadcasted_iota(jnp.int32, (ROWS, 128), 1)
    for i in range(NEAR):
        start = offsets_ref[0, FAR + i]
        base = pl.multiple_of((start // 128) * 128, 128)
        shift = start % 128
        tiles = [
            pltpu.roll(total_ref[:, pl.ds(base + 128 * t, 128)], (128 - shift) % 128, 1)
            for t in range(MOST // 128 + 1)
        ]
        for t in range(MOST // 128):
            out_ref[i, :, 128 * t : 128 * (t + 1)] = jnp.where(lane < 128 - shift, tiles[t], tiles[t + 1])


def deliver(width, offsets, after, *near):
    whole = pl.BlockSpec(memory_space=pltpu.VMEM)
    small = pltpu.CompilerParams(vmem_limit_bytes=8 << 20)
    spread = pl.pallas_call(
        functools.partial(spread_kernel, width),
        out_shape=[jax.ShapeDtypeStruct((ROWS, width), jnp.float32)] * FAR,
        in_specs=[whole, pl.BlockSpec(memory_space=pl.ANY)] + [whole] * CHIPS,
        out_specs=[whole] * FAR,
        scratch_shapes=[pltpu.VMEM((ROWS, BLOCKS + width), jnp.float32)],
        compiler_params=small,
        name=f"spread_{width}",
    )(offsets, after, *near)
    met = [spread[0]] + [lax.ppermute(spread[1 + kind], FSDP, far_pairs(kind)) for kind in range(FAR - 1)]
    return pl.pallas_call(
        functools.partial(window_kernel, width),
        out_shape=jax.ShapeDtypeStruct((NEAR, ROWS, MOST), jnp.float32),
        in_specs=[whole] * (1 + FAR),
        out_specs=whole,
        scratch_shapes=[pltpu.VMEM((ROWS, width + MOST + 128), jnp.float32)],
        compiler_params=small,
        name=f"windows_{width}",
    )(offsets, *met)


def prepare_kernel(place_ref, after_ref, momentum_ref, chosen_ref, table_ref, decayed_ref, listed_ref, sparse_ref, live_ref):
    del after_ref
    live = lax.broadcasted_iota(jnp.int32, (BLOCK, MOST), 1) < place_ref[1]
    decayed = jnp.where(live, momentum_decay * momentum_ref[0], 0.0)
    decayed_ref[...] = decayed
    live_ref[...] = live[:8].astype(jnp.float32)
    coeffs = jnp.dot(table_ref[...], decayed, precision=lax.Precision.HIGHEST, preferred_element_type=jnp.float32)
    chosen = chosen_ref[0]
    bit = jnp.left_shift(jnp.int32(1), chosen & 31)
    low = jnp.sum(jnp.where(chosen < 32, bit, 0), axis=0, keepdims=True)
    high = jnp.sum(jnp.where(chosen < 32, 0, bit), axis=0, keepdims=True)
    number = lax.broadcasted_iota(jnp.int32, (32, MOST), 0)
    listed = jnp.concatenate(
        [jnp.right_shift(jnp.broadcast_to(word, (32, MOST)), number) & 1 for word in (low, high)], axis=0
    )
    listed_ref[...] = listed
    sparse_ref[...] = jnp.where(listed != 0, coeffs, 0.0)


def owner_kernel(parts_ref, decayed_ref, listed_ref, sparse_ref, live_ref, table_ref, back_ref, left_ref, copies_ref):
    gathered = jnp.concatenate([parts_ref[b, c] for c in range(2) for b in range(CHIPS)], axis=0)
    gradient = jnp.where(live_ref[:1, :] != 0, gathered * (1.0 / OWNERS), 0.0)
    coeffs = jnp.dot(table_ref[...], gradient, precision=lax.Precision.HIGHEST, preferred_element_type=jnp.float32)
    sparse = sparse_ref[...] + jnp.where(listed_ref[...] != 0, coeffs, 0.0)
    own = jnp.dot(back_ref[...], sparse, precision=lax.Precision.HIGHEST, preferred_element_type=jnp.float32)
    left_ref[...] = decayed_ref[...] + gradient - own
    for r in range(SIDE):
        copies_ref[r] = own


def add_row_kernel(parts_ref, copies_ref):
    added = jnp.sum(parts_ref[...], axis=0)
    for r in range(SIDE):
        copies_ref[r] = added


def last_kernel(live_ref, left_ref, parts_ref, weights_ref, momentum_out_ref, out_ref):
    momentum_out_ref[0] = left_ref[...]
    update = jnp.sum(parts_ref[...], axis=0) * (1.0 / GROUPS)
    out_ref[...] = jnp.where(live_ref[:1, :] != 0, weights_ref[...] - step_rate * update, 0.0)


def body(partials, owner_blocks, momentum, weights, selected):
    owner = lax.axis_index(FSDP)
    group = lax.axis_index(REP)
    smem = pl.BlockSpec(memory_space=pltpu.SMEM)
    whole = pl.BlockSpec(memory_space=pltpu.VMEM)
    small = pltpu.CompilerParams(vmem_limit_bytes=8 << 20)
    place, branch, offsets = pl.pallas_call(
        plan_kernel,
        out_shape=tuple(jax.ShapeDtypeStruct(shape, jnp.int32) for shape in ((2,), (1,), (8, 128))),
        in_specs=[smem, smem],
        out_specs=(smem, smem, whole),
        compiler_params=pltpu.CompilerParams(vmem_limit_bytes=1 << 20),
        name="plan",
    )(jnp.stack([group, owner]).astype(jnp.int32), owner_blocks)
    partials = partials.reshape(BLOCK, BLOCKS)
    leaving = pl.pallas_call(
        other_half_kernel,
        out_shape=jax.ShapeDtypeStruct((BLOCK // 2, BLOCKS), jnp.float32),
        in_specs=[pl.BlockSpec(memory_space=pl.ANY)],
        out_specs=whole,
        scratch_shapes=[pltpu.SemaphoreType.DMA],
        compiler_params=small,
        name="other_half",
    )(partials)
    received = lax.ppermute(leaving, "core", [(0, 1), (1, 0)])
    tiles = pl.pallas_call(
        add_cores_kernel,
        out_shape=[jax.ShapeDtypeStruct((ROWS, BLOCKS), jnp.float32)] * CHIPS,
        in_specs=[pl.BlockSpec(memory_space=pl.ANY), whole, whole],
        out_specs=[whole] * CHIPS,
        compiler_params=pltpu.CompilerParams(vmem_limit_bytes=8 << 20),
        name="add_cores",
    )(place, partials, received)
    table, back = jnp.asarray(dct_matrix()), jnp.asarray(dct_matrix().T)
    square = jax.ShapeDtypeStruct((BLOCK, MOST), jnp.float32)
    decayed, listed, sparse, live = pl.pallas_call(
        prepare_kernel,
        out_shape=(square, jax.ShapeDtypeStruct((BLOCK, MOST), jnp.int32), square, jax.ShapeDtypeStruct((8, MOST), jnp.float32)),
        grid_spec=pltpu.PrefetchScalarGridSpec(
            num_scalar_prefetch=1,
            grid=(1,),
            in_specs=[
                pl.BlockSpec(memory_space=pl.ANY),
                pl.BlockSpec((1, BLOCK, MOST), lambda i, place: (0, 0, 0)),
                pl.BlockSpec((1, K, MOST), lambda i, place: (place[0], 0, 0)),
                pl.BlockSpec((BLOCK, BLOCK), lambda i, place: (0, 0)),
            ],
            out_specs=[pl.BlockSpec((BLOCK, MOST), lambda i, place: (0, 0))] * 3 + [pl.BlockSpec((8, MOST), lambda i, place: (0, 0))],
        ),
        compiler_params=small,
        name="prepare",
    )(place, tiles[0], momentum, selected, table)
    near = [tiles[0]] + [lax.ppermute(tiles[1 + kind], FSDP, near_pairs(kind)) for kind in range(3)]
    windows = lax.switch(branch[0], [functools.partial(deliver, width) for width in WIDTHS], offsets, sparse, *near)
    blocks = lax.all_to_all(windows, ("zl", "core"), 0, 0, tiled=False).reshape(CHIPS, 2, ROWS, MOST)

    left, copies = pl.pallas_call(
        owner_kernel,
        out_shape=(square, jax.ShapeDtypeStruct((SIDE, BLOCK, MOST), jnp.float32)),
        in_specs=[whole] * 7,
        out_specs=(whole, whole),
        compiler_params=small,
        name="owner_step",
    )(blocks, decayed, listed, sparse, live, table, back)
    row = lax.all_to_all(copies, REP + FSDP, 0, 0, axis_index_groups=rep_groups(0), tiled=False)
    copies = pl.pallas_call(
        add_row_kernel,
        out_shape=jax.ShapeDtypeStruct((SIDE, BLOCK, MOST), jnp.float32),
        in_specs=[whole],
        out_specs=whole,
        compiler_params=pltpu.CompilerParams(vmem_limit_bytes=8 << 20),
        name="add_row",
    )(row)
    everyone = lax.all_to_all(copies, REP + FSDP, 0, 0, axis_index_groups=rep_groups(1), tiled=False)
    new_momentum, new_weights = pl.pallas_call(
        last_kernel,
        out_shape=(jax.ShapeDtypeStruct((1, BLOCK, MOST), jnp.float32), square),
        in_specs=[whole] * 4,
        out_specs=(whole, whole),
        compiler_params=small,
        name="weights_step",
    )(live, left, everyone, weights)
    return new_momentum, new_weights


def solution(mesh):
    fine = Mesh(mesh.devices.reshape(SIDE, SIDE, FAR, CHIPS, 2), REP + FSDP)
    return jax.shard_map(
        body,
        mesh=fine,
        in_specs=(P(REP, FSDP, None, None), P(), P(REP, None, FSDP), P(None, FSDP), P(None, None, FSDP)),
        out_specs=(P(REP, None, FSDP), P(None, FSDP)),
        check_vma=False,
    )
```
